128 devices in a mesh: gx: 16 (over z, x), gy: 8 (over y, core).
Axes of the slice: x: 4, y: 4, z: 4, core: 2. Of those that a mesh axis runs over, the one named last changes fastest.
Arguments:
- potential_warmth: float32 [2304, 30, 3000], P(('gx', 'gy')), may hold values from -6 to 6
- saltiness_anomaly: float32 [2304, 30, 3000], P(('gx', 'gy')), may hold values from -6 to 6
- topmost_thermal_inflow: float32 [2304, 3000], P(('gx', 'gy')), may hold values from -8 to 8
- diffusivity_factor: float32 [29], replicated, may hold values from 0.05 to 5
- place_tile_number: int32 [2304], P(('gx', 'gy')), may hold values from -1 to 2303, as said below
- place_stack_strata: int32 [2304, 3000], P(('gx', 'gy')), may hold values from 0 to 30, as said below
- mesh_stack_strata: int32 [2400, 2880], P('gy', 'gx'), may hold values from 0 to 30, as said below
Outputs:
- temperature_new: float32 [2304, 30, 3000], P(('gx', 'gy'))
- salinity_new: float32 [2304, 30, 3000], P(('gx', 'gy'))
- surface_height: float32 [2400, 2880], P('gy', 'gx')
- misfit_vector: float32 [2400, 2880], P('gy', 'gx')
The draws below stay inside these ranges and needn't reach their ends.
Inputs may be any that keep to these rules, and one draw needn't show every extreme that they name: `place_tile_number`: block (by, bx) has id by * 48 + bx. Every block holding an ocean column (mesh_stack_strata > 0) sits in exactly one slot, no block twice, and unlisted blocks are all land. The device at gx, gy holds only blocks with by // 6 = gy, and at most 2 blocks with the same bx // 3; some device holds exactly 2 such blocks. `place_stack_strata`: entry i * 60 + j of a slot equals mesh_stack_strata at row by * 50 + i, column bx * 60 + j of the slot's block; empty slots hold zeros. `mesh_stack_strata`: zero on land.
All inputs are finite; a program needn't handle non-finite values.
Results may differ from the reference program's by a relative error of at most 0.0003.
Values sent between devices are 32-bit elements; how exact they have to be, the bound alone decides.
A program may use at most 256 MiB of HBM per device.

```python
import math
import jax
import jax.numpy as jnp

TILE_SPAN_EASTWARD = 60
TILE_SPAN_NORTH = 50
KX = 3
KY = 6
SEA_DEPTH_STRATA = 30
ITERS = 3
SLOTS = 18
CAP = 2
PLACES_OVERALL = 2304
NX = 2880
NY = 2400
N_GX = 16
N_GY = 8


def ocean_layout(key):
    blocks_x = NX // TILE_SPAN_EASTWARD
    blocks_y = NY // TILE_SPAN_NORTH
    key_land, key_cols, key_coast, key_order = jax.random.split(key, 4)
    land_blocks = jax.random.randint(key_land, (blocks_y, blocks_x), 0, 4) == 0
    forced_ocean = (jnp.arange(blocks_x) < CAP)[None, :] & (jnp.arange(blocks_y) == 0)[:, None]
    land_blocks = land_blocks & jnp.logical_not(forced_ocean)
    column_depth = jax.random.randint(key_cols, (NY, NX), 1, SEA_DEPTH_STRATA + 1)
    coastal = jax.random.randint(key_coast, (NY, NX), 0, 8) == 0
    column_depth = jnp.where(coastal, 0, column_depth)
    column_depth = column_depth.at[0, 0].set(SEA_DEPTH_STRATA)
    land_cells = jnp.repeat(jnp.repeat(land_blocks, TILE_SPAN_NORTH, axis=0), TILE_SPAN_EASTWARD, axis=1)
    grid_depth = jnp.where(land_cells, 0, column_depth).astype(jnp.int32)
    scores = jax.random.randint(key_order, (N_GY, N_GX), 0, 2 ** 20) * N_GX + jnp.arange(N_GX)[None, :]
    shuffled = jnp.argsort(scores, axis=1).astype(jnp.int32)
    slot_index = jnp.arange(SLOTS)
    shifts = shuffled[:, slot_index // CAP]
    device_x = jnp.arange(N_GX)
    owners = (device_x[:, None, None] - shifts[None, :, :]) % N_GX
    bands = jnp.arange(N_GY)[None, :, None]
    block_col = owners * KX + slot_index % KX
    block_row = bands * KY + slot_index // KX
    is_land = land_blocks[block_row, block_col]
    identity = jnp.where(is_land, -1, block_row * blocks_x + block_col).astype(jnp.int32)
    cell_index = jnp.arange(TILE_SPAN_EASTWARD * TILE_SPAN_NORTH)
    grid_rows = block_row[..., None] * TILE_SPAN_NORTH + cell_index // TILE_SPAN_EASTWARD
    grid_cols = block_col[..., None] * TILE_SPAN_EASTWARD + cell_index % TILE_SPAN_EASTWARD
    slot_depth = jnp.where(is_land[..., None], 0, grid_depth[grid_rows, grid_cols]).astype(jnp.int32)
    return (grid_depth, identity.reshape(-1), slot_depth.reshape(-1, TILE_SPAN_EASTWARD * TILE_SPAN_NORTH))


def draw_place_tile_number(key, part):
    shared = ocean_layout(key)
    return shared[1]


def draw_place_stack_strata(key, part):
    shared = ocean_layout(key)
    return shared[2]


def draw_mesh_stack_strata(key, part):
    shared = ocean_layout(key)
    return shared[0]


def levels(rng, dims, pieces, smallest, high):
    loudness, own = 1.0, jax.random.fold_in(rng, 6)
    for position, blocks in pieces:
        steps = jnp.exp(jax.random.uniform(jax.random.fold_in(own, position), (blocks,), jnp.float32, smallest / len(pieces), high / len(pieces)))
        loudness = loudness * jnp.repeat(steps, dims[position] // blocks).reshape([-1 if axis == position else 1 for axis in range(len(dims))])
    return loudness


def gaussian(own_key, extent, spread, reach, shards=(), dtype=jnp.bfloat16):
    drawn = spread * jax.random.normal(own_key, extent, jnp.float32)
    if shards:
        drawn = drawn * levels(own_key, extent, shards, -0.22, 0.18)
    return jnp.clip(drawn, -reach, reach).astype(dtype)


def setup_inputs(seed: int = 0) -> dict:
    key_of = jax.random.split(jax.random.key(seed), 8)
    return {
        "potential_warmth": gaussian(key_of[0], (PLACES_OVERALL, SEA_DEPTH_STRATA, TILE_SPAN_EASTWARD * TILE_SPAN_NORTH), 1.0, 6.0, ((0, 128),), jnp.float32),
        "saltiness_anomaly": gaussian(key_of[1], (PLACES_OVERALL, SEA_DEPTH_STRATA, TILE_SPAN_EASTWARD * TILE_SPAN_NORTH), 1.0, 6.0, ((0, 128),), jnp.float32),
        "topmost_thermal_inflow": gaussian(key_of[2], (PLACES_OVERALL, TILE_SPAN_EASTWARD * TILE_SPAN_NORTH), 1.5, 8.0, ((0, 128),), jnp.float32),
        "diffusivity_factor": jnp.clip(jnp.exp(jax.random.uniform(key_of[3], (SEA_DEPTH_STRATA - 1,), jnp.float32, math.log(0.05), math.log(5.0))), 0.05, 5.0),
        "place_tile_number": draw_place_tile_number(jax.random.fold_in(key_of[7], 71), 0),
        "place_stack_strata": draw_place_stack_strata(jax.random.fold_in(key_of[7], 71), 0),
        "mesh_stack_strata": draw_mesh_stack_strata(jax.random.fold_in(key_of[7], 71), 0),
    }


HALINE_CONTRACT = 0.8
THERMAL_EXPANSE = 0.6
DAMPING = 0.05


def thomas_vertical_inverse(potential_warmth, saltiness_anomaly, topmost_thermal_inflow, diffusivity_factor, marine_strata_number):
    wet_strata_number = potential_warmth.shape[1]
    coupling = [jnp.where(stratum_position + 1 < marine_strata_number, diffusivity_factor[stratum_position], 0.0).astype(jnp.float32) for stratum_position in range(wet_strata_number - 1)]
    forced = jnp.where(marine_strata_number > 0, topmost_thermal_inflow, 0.0)
    gains = []
    heat_rows = []
    salt_rows = []
    for stratum_position in range(wet_strata_number):
        pivots = jnp.ones(topmost_thermal_inflow.shape, jnp.float32)
        thermal_forcing_part = potential_warmth[:, stratum_position, :]
        salt_term = saltiness_anomaly[:, stratum_position, :]
        if stratum_position == 0:
            thermal_forcing_part = thermal_forcing_part + forced
        if stratum_position + 1 < wet_strata_number:
            pivots = pivots + coupling[stratum_position]
        if stratum_position > 0:
            pivots = pivots + coupling[stratum_position - 1] - coupling[stratum_position - 1] * gains[stratum_position - 1]
            thermal_forcing_part = thermal_forcing_part + coupling[stratum_position - 1] * heat_rows[stratum_position - 1]
            salt_term = salt_term + coupling[stratum_position - 1] * salt_rows[stratum_position - 1]
        if stratum_position + 1 < wet_strata_number:
            gains.append(coupling[stratum_position] / pivots)
        else:
            gains.append(jnp.zeros_like(pivots))
        heat_rows.append(thermal_forcing_part / pivots)
        salt_rows.append(salt_term / pivots)
    heat_out = [heat_rows[wet_strata_number - 1]]
    salt_out = [salt_rows[wet_strata_number - 1]]
    for stratum_position in range(wet_strata_number - 2, -1, -1):
        heat_out.append(heat_rows[stratum_position] + gains[stratum_position] * heat_out[-1])
        salt_out.append(salt_rows[stratum_position] + gains[stratum_position] * salt_out[-1])
    return jnp.stack(heat_out[::-1], axis=1), jnp.stack(salt_out[::-1], axis=1)


def weight_balanced(revised_warmth, revised_saltiness, marine_strata_number):
    running = jnp.zeros(marine_strata_number.shape, jnp.float32)
    layers_out = []
    for stratum_position in range(revised_warmth.shape[1]):
        mass_per_volume = jnp.where(stratum_position < marine_strata_number, HALINE_CONTRACT * revised_saltiness[:, stratum_position, :] - THERMAL_EXPANSE * revised_warmth[:, stratum_position, :], 0.0)
        running = running + mass_per_volume
        layers_out.append(running)
    return jnp.stack(layers_out, axis=1)


def neighbours(field):
    east_side = jnp.roll(field, -1, axis=-1)
    west_side = jnp.roll(field, 1, axis=-1)
    folded = jnp.flip(field[..., -1:, :], axis=-1)
    north_side = jnp.concatenate([field[..., 1:, :], folded], axis=-2)
    south_side = jnp.concatenate([jnp.zeros_like(field[..., :1, :]), field[..., :-1, :]], axis=-2)
    return (east_side, west_side, north_side, south_side)


def reference(potential_warmth, saltiness_anomaly, topmost_thermal_inflow, diffusivity_factor, place_tile_number, place_stack_strata, mesh_stack_strata):
    revised_warmth, revised_saltiness = thomas_vertical_inverse(potential_warmth, saltiness_anomaly, topmost_thermal_inflow, diffusivity_factor, place_stack_strata)
    normal_stress = weight_balanced(revised_warmth, revised_saltiness, place_stack_strata)
    blocks_x = NX // TILE_SPAN_EASTWARD
    blocks_y = NY // TILE_SPAN_NORTH
    block_total = blocks_x * blocks_y
    targets = jnp.where(place_tile_number >= 0, place_tile_number, block_total).astype(jnp.int32)
    placed = jnp.zeros((block_total + 1, SEA_DEPTH_STRATA, TILE_SPAN_EASTWARD * TILE_SPAN_NORTH), jnp.float32).at[targets].set(normal_stress)[:block_total]
    pressure_grid = placed.reshape(blocks_y, blocks_x, SEA_DEPTH_STRATA, TILE_SPAN_NORTH, TILE_SPAN_EASTWARD).transpose(2, 0, 3, 1, 4).reshape(SEA_DEPTH_STRATA, NY, NX)
    depth = mesh_stack_strata.astype(jnp.float32)
    faces = [jnp.minimum(depth, other_depth) for other_depth in neighbours(depth)]
    rhs = jnp.zeros((NY, NX), jnp.float32)
    for stratum_position in range(SEA_DEPTH_STRATA):
        layer_field = pressure_grid[stratum_position]
        for neighbour, face_levels in zip(neighbours(layer_field), faces):
            rhs = rhs + jnp.where(stratum_position < face_levels, neighbour - layer_field, 0.0)
    rhs = rhs / SEA_DEPTH_STRATA
    weights = [face_levels / SEA_DEPTH_STRATA for face_levels in faces]
    damping = jnp.where(depth > 0, DAMPING, 1.0)
    diagonal = damping + weights[0] + weights[1] + weights[2] + weights[3]

    def operate(field):
        result = damping * field
        for neighbour, weight in zip(neighbours(field), weights):
            result = result + weight * (field - neighbour)
        return result

    elevation = jnp.zeros((NY, NX), jnp.float32)
    misfit_vector = rhs
    precond = misfit_vector / diagonal
    direction = precond
    precond_dot = jnp.sum(misfit_vector * precond)
    for iteration in range(ITERS):
        image_field = operate(direction)
        step_size = precond_dot / jnp.sum(direction * image_field)
        elevation = elevation + step_size * direction
        misfit_vector = misfit_vector - step_size * image_field
        precond = misfit_vector / diagonal
        next_dot = jnp.sum(misfit_vector * precond)
        direction = precond + (next_dot / precond_dot) * direction
        precond_dot = next_dot
    return revised_warmth, revised_saltiness, elevation, misfit_vector
```

```python
import functools

import jax
import jax.numpy as jnp
from jax import lax
from jax.experimental import pallas as pl
from jax.experimental.pallas import tpu as pltpu
from jax.sharding import PartitionSpec as P

SPAN_E = 60
SPAN_N = 50
KX = 3
KY = 6
LEVELS = 30
SLOTS = KX * KY
CELLS = SPAN_E * SPAN_N
ROWS = KY * SPAN_N
COLS = KX * SPAN_E
TILES = 24
HALINE = 0.8
THERMAL = 0.6
DAMPING = 0.05

TOP = 16
PLANE = 328
UROWS = TOP + SPAN_N * 8
BLK = 32
EAST = COLS - 128
MESH = pl.DeviceIdType.MESH
F32 = jnp.float32
I32 = jnp.int32
VMEM = pltpu.VMEM


def iota(shape, dim):
    return lax.broadcasted_iota(I32, shape, dim)


def lroll(x, shift):
    shift = shift % x.shape[1]
    return x if shift == 0 else pltpu.roll(x, shift, 1)


def sroll(x, shift):
    shift = shift % x.shape[0]
    return x if shift == 0 else pltpu.roll(x, shift, 0)


def lreverse(x):
    lane = iota(x.shape, 1)
    bit = 1
    while bit < 128:
        x = jnp.where((lane & bit) != 0, lroll(x, bit), lroll(x, -bit))
        bit *= 2
    return x


def flip_cols(a, b):
    ra, rb = lreverse(b), lreverse(a)
    shift = 256 - COLS
    lane = iota(a.shape, 1)
    xa, xb = lroll(ra, -shift), lroll(rb, -shift)
    return jnp.where(lane < 128 - shift, xa, xb), jnp.where(lane < 128 - shift, xb, xa)


def barrier(peers):
    sem = pltpu.get_barrier_semaphore()
    for peer in peers:
        pl.semaphore_signal(sem, inc=1, device_id=peer, device_id_type=MESH)
    pl.semaphore_wait(sem, len(peers))


def strips_kernel(n, ng, cap, ids_ref, depth_ref, all_ref, tab_ref, pa, pb, msg, edge, got,
                  s1, r1, s2, r2):
    g = lax.axis_index("gx")
    y = lax.axis_index("gy")
    up, down = lax.rem(y + 1, ng), lax.rem(y + ng - 1, ng)
    barrier([(lax.rem(g + k, n), y) for k in range(1, n)] + [(g, up), (g, down)])
    pa[0:ROWS, :] = depth_ref[:, 0:128]
    pb[0:ROWS, 0:EAST] = depth_ref[:, 128:COLS]
    lane = iota((8, 128), 1)
    strips = [[jnp.zeros((8, 128), I32) for _ in range(2)] for _ in range(KX)]
    ns = []
    for i in range(SPAN_N):
        off = SPAN_E * i % 128
        a = pa[pl.ds(i, 8, stride=SPAN_N), :]
        b = pb[pl.ds(i, 8, stride=SPAN_N), :]
        cells = [a, a, jnp.where(lane < 64, b, a)]
        here = (lane == off) | (lane == (off + SPAN_E - 1) % 128)
        for bx in range(KX):
            strips[bx][i // 32] = jnp.where(here, lroll(cells[bx], off - SPAN_E * bx), strips[bx][i // 32])
        if i == 0:
            ns = [lroll(cells[bx], -SPAN_E * bx) for bx in range(KX)]
        if i == SPAN_N - 1:
            ns = [
                jnp.where(lane < SPAN_E, ns[bx], lroll(cells[bx], SPAN_E - SPAN_E * bx))
                for bx in range(KX)
            ]
    for bx in range(KX):
        for part, value in enumerate((strips[bx][0], strips[bx][1], ns[bx])):
            msg[pl.ds(bx * 3 + part, 8, stride=9), :] = value
    edge[...] = jnp.zeros((8, 128), I32)
    for bx in range(KX):
        edge[bx : bx + 1, :] = ns[bx][0:1]
        edge[3 + bx : 4 + bx, :] = ns[bx][KY - 1 : KY]
    copies = []
    for slot, target in ((0, up), (1, down)):
        copy = pltpu.make_async_remote_copy(
            edge, got.at[slot], s1.at[slot], r1.at[slot], device_id=(g, target), device_id_type=MESH
        )
        copy.start()
        copies.append(copy)
    row = iota((1, 128), 1)
    code = jnp.full((1, 128), -1, I32)
    owners = []
    for s in range(SLOTS):
        block = jnp.maximum(ids_ref[s], 0)
        bx = lax.rem(block, KX * n)
        by = lax.rem(lax.div(block, KX * n), KY)
        owner = jnp.where(ids_ref[s] >= 0, lax.div(bx, KX), -1)
        rank = jnp.int32(0)
        for other in owners:
            rank = rank + jnp.where(other == owner, 1, 0)
        owners.append(owner)
        value = (owner * 32 + by * KX + lax.rem(bx, KX)) * 32 + rank
        code = jnp.where(row == s, jnp.where(owner >= 0, value, -1), code)
    msg[54:55, :] = code
    for bx, place in enumerate((55, 62, 63)):
        msg[place : place + 1, :] = lroll(lreverse(ns[bx]), -8)[KY - 1 : KY]
    for copy in copies:
        copy.wait()
    msg[56:59, :] = got[1][0:3]
    msg[59:62, :] = got[0][3:6]
    copies = []
    for k in range(1, n):
        target = lax.rem(g + k, n)
        copy = pltpu.make_async_remote_copy(
            msg.at[pl.ds(0, 64)], all_ref.at[g], s2.at[k], r2.at[k], device_id=(target, y), device_id_type=MESH
        )
        copy.start()
        copies.append(copy)
    all_ref[pl.ds(g, 1)] = msg[0:64, :][None]
    for copy in copies:
        copy.wait()
    codes = all_ref[:, 54, :]
    key = codes >> 5
    rank = codes & 31
    source = iota((n, 128), 0)
    number = (source * cap + rank + 1).astype(F32)
    for p in range(SLOTS):
        hit = jnp.where(key == g * 32 + p, number, 0.0)
        hit = jnp.sum(jnp.sum(hit, axis=0, keepdims=True), axis=1, keepdims=True)
        tab_ref[p : p + 1, :] = jnp.broadcast_to(hit.astype(I32) - 1, (1, 128))
    tab_ref[SLOTS:24, :] = jnp.full((24 - SLOTS, 128), -1, I32)


def ahead(x, step):
    a = lroll(x, -step)
    return jnp.where(iota(x.shape, 1) < 128 - step, a, sroll(a, -1))


def behind(x, step):
    a = lroll(x, step)
    return jnp.where(iota(x.shape, 1) >= step, a, sroll(a, 1))


def columns_kernel(n, ng, cap, ids_ref, dfac_ref, flux_ref, depth_ref, strips_ref, heat_ref, salt_ref,
                   heat_out, salt_out, msg_ref, nflat, fflat, coef, jcol, inh, ins, yh, ys, oh, os_, count):
    step = pl.program_id(0)
    shape = (TILES, 128)
    row24 = iota(shape, 0)
    lane24 = iota(shape, 1)
    cell = row24 * 128 + lane24
    lane = iota((1, 128), 1)
    last = CELLS - 128 * (TILES - 1)

    @pl.when(step == 0)
    def _():
        for t in range(TILES):
            width = 128 if t < TILES - 1 else last
            cols = slice(t * 128, t * 128 + width)
            for first in (0, 8, 16):
                rows = min(8, SLOTS - first)
                place = pl.ds(first * TILES + t, rows, stride=TILES)
                d = depth_ref[first : first + rows, cols]
                f = flux_ref[first : first + rows, cols]
                if width < 128:
                    d = jnp.concatenate([d, jnp.zeros((rows, 128 - width), I32)], axis=1)
                    f = jnp.concatenate([f, jnp.zeros((rows, 128 - width), F32)], axis=1)
                nflat[place, :] = d
                fflat[place, :] = f
        gain = jnp.zeros((1, 128), F32)
        for k in range(LEVELS):
            above = dfac_ref[k - 1] if k > 0 else jnp.float32(0)
            below = dfac_ref[k] if k + 1 < LEVELS else jnp.float32(0)
            base = (1.0 + above) - above * gain
            full = 1.0 / (base + below)
            gain = below * full
            coef[0, k : k + 1, :] = full
            coef[1, k : k + 1, :] = 1.0 / base
            coef[2, k : k + 1, :] = jnp.broadcast_to(above, (1, 128))
            coef[3, k : k + 1, :] = gain
        owner = cell.astype(F32)
        whole = jnp.floor((owner + 0.5) * (1.0 / SPAN_E))
        jcol[...] = cell - whole.astype(I32) * SPAN_E
        for d in range(n):
            count[d] = 0

    for t in range(TILES):
        width = 128 if t < TILES - 1 else last
        cols = slice(t * 128, t * 128 + width)
        inh[t * 32 : t * 32 + LEVELS, 0:width] = heat_ref[0, :, cols]
        ins[t * 32 : t * 32 + LEVELS, 0:width] = salt_ref[0, :, cols]

    mine = pl.ds(pl.multiple_of(step * TILES, 8), TILES)
    depth = nflat[mine, :]
    wet = depth > 0
    h = s = None
    for k in range(LEVELS):
        level = pl.ds(k, TILES, stride=32)
        rh = inh[level, :]
        rs = ins[level, :]
        deeper = depth > k + 1
        if k == 0:
            rh = rh + jnp.where(wet, fflat[mine, :], 0.0)
            pivot = jnp.where(deeper, coef[0, 0:1, :], 1.0)
            h = rh * pivot
            s = rs * pivot
        else:
            above = jnp.where(wet, coef[2, k : k + 1, :], 0.0)
            pivot = jnp.where(wet, coef[1, k : k + 1, :], 1.0)
            if k + 1 < LEVELS:
                pivot = jnp.where(deeper, coef[0, k : k + 1, :], pivot)
            h = (rh + above * h) * pivot
            s = (rs + above * s) * pivot
        if k + 1 < LEVELS:
            yh[k * TILES : (k + 1) * TILES, :] = h
            ys[k * TILES : (k + 1) * TILES, :] = s
        wet = deeper
    level = pl.ds(LEVELS - 1, TILES, stride=32)
    oh[level, :] = h
    os_[level, :] = s
    for k in range(LEVELS - 2, -1, -1):
        gain = jnp.where(depth > k + 1, coef[3, k : k + 1, :], 0.0)
        h = yh[k * TILES : (k + 1) * TILES, :] + gain * h
        s = ys[k * TILES : (k + 1) * TILES, :] + gain * s
        level = pl.ds(k, TILES, stride=32)
        oh[level, :] = h
        os_[level, :] = s
    for t in range(TILES):
        width = 128 if t < TILES - 1 else last
        cols = slice(t * 128, t * 128 + width)
        heat_out[0, :, cols] = oh[t * 32 : t * 32 + LEVELS, 0:width]
        salt_out[0, :, cols] = os_[t * 32 : t * 32 + LEVELS, 0:width]

    blocks_x = KX * n
    ident = ids_ref[step]
    block = jnp.maximum(ident, 0)
    bx = lax.rem(block, blocks_x)
    by = lax.div(block, blocks_x)
    byl = lax.rem(by, KY)
    dev = lax.div(bx, KX)
    bxl = lax.rem(bx, KX)

    def strip(device, place):
        return strips_ref[device, pl.ds(place, 1), :]

    def sides(col, part):
        return strip(lax.div(col, KX), (byl * KX + lax.rem(col, KX)) * 3 + part)

    east = lax.rem(bx + 1, blocks_x)
    west = lax.rem(bx + blocks_x - 1, blocks_x)
    ew = [
        jnp.where((lane & 3) == 3, lroll(sides(east, part), SPAN_E - 1), lroll(sides(west, part), 1 - SPAN_E))
        for part in range(2)
    ]
    ew = jnp.where(row24 < 15, ew[0], ew[1])
    mirror = blocks_x - 1 - bx
    mirrored = lax.rem(mirror, KX)
    folded = by == KY * ng - 1
    inner = byl < KY - 1
    north_dev = jnp.where(folded, lax.div(mirror, KX), dev)
    north_row = jnp.where(
        inner,
        ((byl + 1) * KX + bxl) * 3 + 2,
        jnp.where(folded, jnp.where(mirrored == 0, 55, 61 + mirrored), 56 + bxl),
    )
    north = lroll(strip(north_dev, north_row), -4)
    south_row = jnp.where(byl > 0, ((byl - 1) * KX + bxl) * 3 + 2, 59 + bxl)
    south = jnp.where(by > 0, lroll(strip(dev, south_row), -SPAN_E), 0)
    j = jcol[...]
    inside = cell < CELLS
    first_j = j == 0
    last_j = j == SPAN_E - 1
    first_i = cell < SPAN_E
    last_i = cell >= CELLS - SPAN_E
    faces = (
        jnp.minimum(depth, jnp.where(last_j, ew, ahead(depth, 1))),
        jnp.minimum(depth, jnp.where(first_j, ew, behind(depth, 1))),
        jnp.minimum(depth, jnp.where(last_i, north, ahead(depth, SPAN_E))),
        jnp.minimum(depth, jnp.where(first_i, south, behind(depth, SPAN_E))),
    )
    sums = [jnp.zeros(shape, F32) for _ in range(4)]
    pressure = jnp.zeros(shape, F32)
    total = jnp.zeros(shape, F32)
    for k in range(LEVELS):
        level = pl.ds(k, TILES, stride=32)
        pressure = pressure + (HALINE * os_[level, :] - THERMAL * oh[level, :])
        total = total + pressure
        sums = [jnp.where(face == k + 1, total, held) for face, held in zip(faces, sums)]
    sums = [jnp.where(inside, held, 0.0) for held in sums]
    se, sw, sn, ss = sums
    local = jnp.where(last_j, 0.0, ahead(sw, 1)) - se
    local = local + (jnp.where(first_j, 0.0, behind(se, 1)) - sw)
    local = local + (jnp.where(last_i, 0.0, ahead(ss, SPAN_E)) - sn)
    local = local + (jnp.where(first_i, 0.0, behind(sn, SPAN_E)) - ss)
    local = jnp.where(inside, local, 0.0)
    rim = jnp.where(last_j, se, jnp.where(first_j, sw, 0.0))
    rim0 = jnp.sum(jnp.where(row24 < 15, rim, 0.0), axis=0, keepdims=True)
    rim1 = jnp.sum(jnp.where(row24 >= 15, rim, 0.0), axis=0, keepdims=True)
    top = jnp.sum(jnp.where(last_i, sn, 0.0), axis=0, keepdims=True)
    bottom = jnp.sum(jnp.where(first_i, ss, 0.0), axis=0, keepdims=True)
    cap_row = jnp.where(lane < SPAN_E, bottom, jnp.where(lane < 2 * SPAN_E, lroll(top, 64), 0.0))

    @pl.when(ident >= 0)
    def _():
        rank = count[dev]
        count[dev] = rank + 1
        msg_ref[dev, pl.ds(pl.multiple_of(rank * TILES, 8), TILES), :] = local
        base = cap * TILES + rank * 3
        for part, value in enumerate((rim0, rim1, cap_row)):
            msg_ref[dev, pl.ds(base + part, 1), :] = value


def barotropic_kernel(n, ng, cap, tab_ref, depth_ref, msg_ref, height_ref, misfit_ref,
                      recv, blk, dpl, upl, zpl, wts, qpl, row_out, row_in, col_out, col_in,
                      red_out, red_x, red_y, own_sem, a2a_s, a2a_r, row_s, row_r, col_s, col_r,
                      rx_s, rx_r, ry_s, ry_r):
    g = lax.axis_index("gx")
    y = lax.axis_index("gy")
    band = [(lax.rem(g + k, n), y) for k in range(1, n)]
    column = [(g, lax.rem(y + k, ng)) for k in range(1, ng)]
    barrier(band + column)
    own = pltpu.make_async_copy(msg_ref.at[g], recv.at[g], own_sem)
    own.start()
    sends = []
    for k, peer in enumerate(band):
        copy = pltpu.make_async_remote_copy(
            msg_ref.at[peer[0]], recv.at[g], a2a_s.at[k], a2a_r.at[k], device_id=peer, device_id_type=MESH
        )
        copy.start()
        sends.append(copy)

    lane = iota((8, 128), 1)
    sub = iota((8, 128), 0)
    at_top = lax.div(y + 1, ng)
    is_top = y == ng - 1
    has_south = y > 0

    def rows_start(k, north, north_folded, south):
        flipped = flip_cols(*north_folded)
        for half in range(2):
            row_out[k, 0, half] = jnp.where(is_top, flipped[half], north[half])
            row_out[k, 1, half] = south[half]
        up = pltpu.make_async_remote_copy(
            row_out.at[k, 0], row_in.at[k, at_top], row_s.at[k, 0], row_r.at[k, at_top],
            device_id=(g + at_top * (n - 1 - 2 * g), y + 1 - at_top), device_id_type=MESH,
        )
        down = pltpu.make_async_remote_copy(
            row_out.at[k, 1], row_in.at[k, 1], row_s.at[k, 1], row_r.at[k, 1],
            device_id=(g, lax.rem(y + ng - 1, ng)), device_id_type=MESH,
        )
        up.start()

        @pl.when(has_south)
        def _():
            down.start()

        return up, down

    def rows_wait(k, up, down):
        up.wait_send()

        @pl.when(has_south)
        def _():
            down.wait_send()
            south = pltpu.make_async_remote_copy(
                row_out.at[k, 1], row_in.at[k, 0], row_s.at[k, 1], row_r.at[k, 0],
                device_id=(g, lax.rem(y + ng - 1, ng)), device_id_type=MESH,
            )
            south.wait_recv()

        down.wait_recv()

        @pl.when(jnp.logical_not(has_south))
        def _():
            row_in[k, 0] = jnp.zeros((2, 8, 128), F32)

        return [row_in[k, 0, half] for half in range(2)], [row_in[k, 1, half] for half in range(2)]

    def cols_start(k):
        copies = []
        for slot, target in ((0, lax.rem(g + 1, n)), (1, lax.rem(g + n - 1, n))):
            copy = pltpu.make_async_remote_copy(
                col_out.at[k, slot], col_in.at[k, slot], col_s.at[k, slot], col_r.at[k, slot],
                device_id=(target, y), device_id_type=MESH,
            )
            copy.start()
            copies.append(copy)
        return copies

    def halo(k, plane):
        north = [plane[half, 312:320, :] for half in range(2)]
        south = [plane[half, 16:24, :] for half in range(2)]
        turned = [
            jnp.where(sub == 0, sroll(v, -3), jnp.where(sub == 1, sroll(v, -1), sroll(v, 1))) for v in north
        ]
        below, above = rows_wait(k, *rows_start(k, north, turned, south))
        for half in range(2):
            plane[half, 8:16, :] = sroll(below[half], 4)
            plane[half, 312:320, :] = jnp.where(sub < 4, north[half], sroll(above[half], 4))
        to_east = jnp.zeros((8, 128), F32)
        to_west = jnp.zeros((8, 128), F32)
        for t in range(39):
            here = (lane >= 3 * t) & (lane < 3 * t + 3)
            rows = slice(8 + 8 * t, 16 + 8 * t)
            to_east = jnp.where(here, lroll(plane[1, rows, :], 3 * t - (EAST - 3)), to_east)
            to_west = jnp.where(here, lroll(plane[0, rows, :], 3 * t), to_west)
        col_out[k, 0, 0:8, :] = to_east
        col_out[k, 1, 0:8, :] = to_west
        for copy in cols_start(k):
            copy.wait()
        from_west = col_in[k, 0, 0:8, :]
        from_east = col_in[k, 1, 0:8, :]
        for t in range(39):
            rows = slice(8 + 8 * t, 16 + 8 * t)
            plane[1, rows, :] = jnp.where(
                lane >= 125,
                lroll(from_west, 125 - 3 * t),
                jnp.where((lane >= EAST) & (lane < EAST + 3), lroll(from_east, EAST - 3 * t), plane[1, rows, :]),
            )

    zero8 = jnp.zeros((8, 128), F32)
    for half in range(2):
        dpl[half, 0:16, :] = jnp.zeros((16, 128), F32)
        dpl[half, 312:PLANE, :] = jnp.zeros((PLANE - 312, 128), F32)
    dpl[0, TOP : TOP + ROWS, :] = depth_ref[:, 0:128].astype(F32)
    dpl[1, TOP : TOP + ROWS, :] = jnp.zeros((ROWS, 128), F32)
    dpl[1, TOP : TOP + ROWS, 0:EAST] = depth_ref[:, 128:COLS].astype(F32)
    for half in range(2):
        for ref in (zpl, qpl.at[0], qpl.at[1], qpl.at[2], qpl.at[3]):
            ref[half, 0:8, :] = zero8
            ref[half, 320:PLANE, :] = zero8
    halo(0, dpl)

    span = 24
    chunks = 13
    lane_c = iota((span, 128), 1)

    def rows_at(t, shift=0):
        return pl.ds(8 + t * span + shift, span)

    def both(ref, rows):
        return [ref[half, rows, :] for half in range(2)]

    def from_east(pair):
        a, b = [lroll(v, -1) for v in pair]
        return jnp.where(lane_c < 127, a, b), jnp.where(lane_c < 127, b, a)

    def from_west(pair):
        a, b = [lroll(v, 1) for v in pair]
        return jnp.where(lane_c >= 1, a, b), jnp.where(lane_c >= 1, b, a)

    def weigh(t, carry):
        rows = rows_at(t)
        d = both(dpl, rows)
        beside = (from_east(d), from_west(d), both(dpl, rows_at(t, 1)), both(dpl, rows_at(t, -1)))
        r = iota((span, 128), 0) + (8 + t * span)
        for half in range(2):
            damp = jnp.where(d[half] > 0, DAMPING, 1.0)
            diagonal = damp
            for side in range(4):
                w = jnp.minimum(d[half], beside[side][half]) * (1.0 / LEVELS)
                wts[side, half, rows, :] = w
                diagonal = diagonal + w
            inverse = 1.0 / diagonal
            wts[4, half, rows, :] = damp
            wts[5, half, rows, :] = inverse
            inside = (r >= TOP) & (r < TOP + ROWS)
            if half == 1:
                inside = inside & (lane_c < EAST)
            wts[6, half, rows, :] = jnp.where(inside, inverse, 0.0)
        return carry

    lax.fori_loop(0, chunks, weigh, 0)

    own.wait()
    for copy in sends:
        copy.wait()
    for bx in range(KX):
        blk[(bx * 8 + KY) * BLK : (bx + 1) * 8 * BLK, :] = jnp.zeros((2 * BLK, 128), F32)
        wanted = [
            jnp.broadcast_to(tab_ref[by * KX + bx : by * KX + bx + 1, :], (8, 128)) for by in range(KY)
        ]

        def pick(source, held, wanted=wanted):
            held = list(held)
            for rank in range(cap):
                parts = [recv[source, rank * TILES + 8 * v : rank * TILES + 8 * v + 8, :] for v in range(3)]
                first = cap * TILES + rank * 3
                rest = recv[source, first : first + 3, :]
                for by in range(KY):
                    hit = wanted[by] == source * cap + rank
                    for v in range(3):
                        held[by * 4 + v] = jnp.where(hit, parts[v], held[by * 4 + v])
                    held[by * 4 + 3] = jnp.where(hit[0:3], rest, held[by * 4 + 3])
            return tuple(held)

        start = ([zero8] * 3 + [jnp.zeros((3, 128), F32)]) * KY
        held = lax.fori_loop(0, n, pick, tuple(start))
        for by in range(KY):
            base = (bx * 8 + by) * BLK
            for v in range(3):
                blk[base + 8 * v : base + 8 * v + 8, :] = held[by * 4 + v]
            blk[base + TILES : base + TILES + 3, :] = held[by * 4 + 3]

    def rows_of(bx, row):
        return blk[pl.ds(bx * 8 * BLK + row, 8, stride=BLK), :]

    rims = [[rows_of(bx, TILES + part) for part in range(2)] for bx in range(KX)]
    for part in range(2):
        col_out[1, 0, 8 * part : 8 * part + 8, :] = rims[KX - 1][part]
        col_out[1, 1, 8 * part : 8 * part + 8, :] = rims[0][part]
    cap_rows = [rows_of(bx, TILES + 2) for bx in range(KX)]

    def lay(v):
        tail = jnp.where(lane < EAST, v[2], 0.0)
        return jnp.where(lane < 60, v[0], jnp.where(lane < 120, v[1], v[2])), tail

    souths = lay([lroll(cap_rows[bx], SPAN_E * bx) for bx in range(KX)])
    norths = lay([lroll(cap_rows[bx], SPAN_E * bx - SPAN_E) for bx in range(KX)])
    waits = rows_start(1, norths, [sroll(v, 8 - (KY - 1)) for v in norths], souths)
    col_copies = cols_start(1)
    for i in range(SPAN_N):
        t, off = SPAN_E * i // 128, SPAN_E * i % 128
        cells = []
        for bx in range(KX):
            value = rows_of(bx, t)
            if off + SPAN_E > 128:
                value = jnp.where(lane >= off, value, rows_of(bx, t + 1))
            cells.append(lroll(value, SPAN_E * bx - off))
        first, second = lay(cells)
        rim = [rims[bx][i // 32] for bx in range(KX)]
        first = first + jnp.where(
            lane == 59,
            lroll(rim[1], 59 - off),
            jnp.where(
                lane == 60,
                lroll(rim[0], 1 - off),
                jnp.where(lane == 119, lroll(rim[2], 119 - off), jnp.where(lane == 120, lroll(rim[1], 61 - off), 0.0)),
            ),
        )
        if i == SPAN_N - 1:
            first = first + jnp.where(sub < KY - 1, sroll(souths[0], -1), 0.0)
            second = second + jnp.where(sub < KY - 1, sroll(souths[1], -1), 0.0)
        if i == 0:
            first = first + jnp.where((sub > 0) & (sub < KY), sroll(norths[0], 1), 0.0)
            second = second + jnp.where((sub > 0) & (sub < KY), sroll(norths[1], 1), 0.0)
        upl[0, pl.ds(TOP + i, 8, stride=SPAN_N), :] = first
        upl[1, pl.ds(TOP + i, 8, stride=SPAN_N), :] = second
    below, above = rows_wait(1, *waits)
    for copy in col_copies:
        copy.wait()
    for half in range(2):
        upl[half, TOP : TOP + 1, :] = upl[half, TOP : TOP + 1, :] + below[half][KY - 1 : KY]
        end = TOP + ROWS - 1
        upl[half, end : end + 1, :] = upl[half, end : end + 1, :] + above[half][0:1]
        upl[half, 8:16, :] = zero8
    for i in range(SPAN_N):
        off = SPAN_E * i % 128
        part = slice(8 * (i // 32), 8 * (i // 32) + 8)
        rows = pl.ds(TOP + i, 8, stride=SPAN_N)
        west = lroll(col_in[1, 0, part, :], 1 - SPAN_E - off)
        east = lroll(col_in[1, 1, part, :], COLS - 1 - off)
        good = sub < KY
        upl[0, rows, :] = upl[0, rows, :] + jnp.where((lane == 0) & good, west, 0.0)
        upl[1, rows, :] = upl[1, rows, :] + jnp.where((lane == EAST - 1) & good, east, 0.0)

    def begin(t, carry):
        rows = rows_at(t)
        for half in range(2):
            rhs = upl[half, rows, :] * (1.0 / LEVELS)
            qpl[0, half, rows, :] = rhs
            zpl[half, rows, :] = rhs * wts[5, half, rows, :]
        return carry

    lax.fori_loop(0, chunks, begin, 0)
    halo(2, zpl)

    def image(out, scale_next):
        def body(t, carry):
            rows = rows_at(t)
            v = both(zpl, rows)
            beside = (from_east(v), from_west(v), both(zpl, rows_at(t, 1)), both(zpl, rows_at(t, -1)))
            for half in range(2):
                result = wts[4, half, rows, :] * v[half]
                for side in range(4):
                    result = result + wts[side, half, rows, :] * (v[half] - beside[side][half])
                qpl[out, half, rows, :] = result
            return carry

        lax.fori_loop(0, chunks, body, 0)
        if scale_next:

            def scale(t, carry):
                rows = rows_at(t)
                for half in range(2):
                    zpl[half, rows, :] = qpl[out, half, rows, :] * wts[5, half, rows, :]
                return carry

            lax.fori_loop(0, chunks, scale, 0)

    def everywhere(k, parts):
        red_out[k, 0] = zero8
        for place, part in enumerate(parts):
            red_out[k, 0, place : place + 1, :] = jnp.sum(part, axis=0, keepdims=True)
        for level, (peers, into, sem_s, sem_r, me) in enumerate(
            ((band, red_x, rx_s, rx_r, g), (column, red_y, ry_s, ry_r, y))
        ):
            copies = []
            for number, peer in enumerate(peers):
                copy = pltpu.make_async_remote_copy(
                    red_out.at[k, level], into.at[k, me], sem_s.at[k, number], sem_r.at[k, number],
                    device_id=peer, device_id_type=MESH,
                )
                copy.start()
                copies.append(copy)
            into[k, pl.ds(me, 1)] = red_out[k, level][None]
            for copy in copies:
                copy.wait()
            total = jnp.sum(into[k], axis=0)
            if level == 0:
                red_out[k, 1] = total
        total = jnp.sum(total, axis=1, keepdims=True)
        return [jnp.broadcast_to(total[place : place + 1], (8, 128)) for place in range(len(parts))]

    image(1, True)

    def first_dots(t, carry):
        rows = rows_at(t)
        a, b = carry
        for half in range(2):
            z = qpl[0, half, rows, :] * wts[6, half, rows, :]
            a = a + qpl[0, half, rows, :] * z
            b = b + qpl[1, half, rows, :] * z
        return a, b

    zero_c = jnp.zeros((span, 128), F32)
    mu = everywhere(0, lax.fori_loop(0, chunks, first_dots, (zero_c, zero_c)))
    image(2, True)
    image(3, False)
    norm = mu[0]
    ray = mu[1] / norm
    ray_c = jnp.broadcast_to(ray[0:1], (span, 128))

    def shift(t, carry):
        rows = rows_at(t)
        c = list(carry)
        for half in range(2):
            w0, w1, w2, w3 = [qpl[j, half, rows, :] for j in range(4)]
            q1 = w1 - ray_c * w0
            t2 = w2 - ray_c * w1
            t3 = (w3 - ray_c * w2) - ray_c * t2
            q2 = t2 - ray_c * q1
            q3 = t3 - ray_c * q2
            qpl[1, half, rows, :] = q1
            qpl[2, half, rows, :] = q2
            qpl[3, half, rows, :] = q3
            inverse = wts[6, half, rows, :]
            z1 = q1 * inverse
            z2 = q2 * inverse
            c[0] = c[0] + w0 * z1
            c[1] = c[1] + q1 * z1
            c[2] = c[2] + q2 * z1
            c[3] = c[3] + q2 * z2
            c[4] = c[4] + q3 * z2
        return tuple(c)

    moment = everywhere(1, lax.fori_loop(0, chunks, shift, (zero_c,) * 5))
    one = jnp.ones((8, 128), F32)
    scale = one / norm
    c = [one] + [m * scale for m in moment]
    zero = zero8
    rho = [one, zero, zero, zero]
    pi = [one, zero, zero]
    xs = [zero, zero, zero]
    gamma = one
    for it in range(3):
        curve = zero
        for i in range(it + 1):
            for j in range(it + 1):
                curve = curve + (pi[i] * pi[j]) * (ray * c[i + j] + c[i + j + 1])
        alpha = gamma / curve
        xs = [xs[i] + alpha * pi[i] if i <= it else xs[i] for i in range(3)]
        for i in range(it + 2):
            step = ray * pi[i] if i <= it else zero
            if i > 0:
                step = step + pi[i - 1]
            rho[i] = rho[i] - alpha * step
        if it == 2:
            break
        gamma_new = zero
        for i in range(it + 2):
            for j in range(it + 2):
                gamma_new = gamma_new + (rho[i] * rho[j]) * c[i + j]
        beta = gamma_new / gamma
        pi = [rho[i] + beta * pi[i] for i in range(3)]
        gamma = gamma_new

    def finish(first, size):
        rows = pl.ds(TOP + first, size)
        out = pl.ds(first, size)
        x = [jnp.broadcast_to(v[0:1], (size, 128)) for v in xs]
        r = [jnp.broadcast_to(v[0:1], (size, 128)) for v in rho]
        for half in range(2):
            q = [qpl[j, half, rows, :] for j in range(4)]
            high = (x[0] * q[0] + x[1] * q[1] + x[2] * q[2]) * wts[5, half, rows, :]
            rest = r[0] * q[0] + r[1] * q[1] + r[2] * q[2] + r[3] * q[3]
            if half == 0:
                height_ref[out, 0:128] = high
                misfit_ref[out, 0:128] = rest
            else:
                height_ref[out, 128:COLS] = high[:, 0:EAST]
                misfit_ref[out, 128:COLS] = rest[:, 0:EAST]

    def finish_chunk(t, carry):
        finish(pl.multiple_of(t * span, 8), span)
        return carry

    lax.fori_loop(0, ROWS // span, finish_chunk, 0)
    finish(ROWS // span * span, ROWS % span)


def on_device(n, ng, heat, salt, flux, dfac, ids, slot_depth, grid_depth):
    cap = (SLOTS + n - 1) // n
    msg_rows = cap * TILES + (cap * 3 + 7) // 8 * 8
    vmem = pl.BlockSpec(memory_space=VMEM)
    smem = pl.BlockSpec(memory_space=pltpu.SMEM)
    dma = pltpu.SemaphoreType.DMA
    big = 56 * 2**20
    strips, table = pl.pallas_call(
        functools.partial(strips_kernel, n, ng, cap),
        out_shape=(jax.ShapeDtypeStruct((n, 64, 128), I32), jax.ShapeDtypeStruct((24, 128), I32)),
        in_specs=[smem, vmem],
        out_specs=(vmem, vmem),
        scratch_shapes=[
            VMEM((400, 128), I32), VMEM((400, 128), I32), VMEM((72, 128), I32), VMEM((8, 128), I32),
            VMEM((2, 8, 128), I32), dma((2,)), dma((2,)), dma((n,)), dma((n,)),
        ],
        compiler_params=pltpu.CompilerParams(collective_id=0, has_side_effects=True, vmem_limit_bytes=big),
        name="strips",
    )(ids, grid_depth)

    whole = lambda s: (0, 0)
    block = pl.BlockSpec((1, LEVELS, CELLS), lambda s: (s, 0, 0))
    heat_new, salt_new, msg = pl.pallas_call(
        functools.partial(columns_kernel, n, ng, cap),
        grid=(SLOTS,),
        out_shape=(
            jax.ShapeDtypeStruct(heat.shape, F32),
            jax.ShapeDtypeStruct(salt.shape, F32),
            jax.ShapeDtypeStruct((n, msg_rows, 128), F32),
        ),
        in_specs=[
            smem, smem,
            pl.BlockSpec((SLOTS, CELLS), whole),
            pl.BlockSpec((SLOTS, CELLS), whole),
            pl.BlockSpec((n, 64, 128), lambda s: (0, 0, 0)),
            block, block,
        ],
        out_specs=(block, block, pl.BlockSpec((n, msg_rows, 128), lambda s: (0, 0, 0))),
        scratch_shapes=[
            VMEM((SLOTS * TILES, 128), I32), VMEM((SLOTS * TILES, 128), F32), VMEM((4, 32, 128), F32),
            VMEM((TILES, 128), I32),
            VMEM((TILES * 32, 128), F32), VMEM((TILES * 32, 128), F32),
            VMEM((TILES * LEVELS, 128), F32), VMEM((TILES * LEVELS, 128), F32),
            VMEM((TILES * 32, 128), F32), VMEM((TILES * 32, 128), F32),
            pltpu.SMEM((n,), I32),
        ],
        compiler_params=pltpu.CompilerParams(vmem_limit_bytes=big),
        name="columns",
    )(ids, dfac, flux, slot_depth, strips, heat, salt)

    field = jax.ShapeDtypeStruct((ROWS, COLS), F32)
    plane = (2, PLANE, 128)
    height, misfit = pl.pallas_call(
        functools.partial(barotropic_kernel, n, ng, cap),
        out_shape=(field, field),
        in_specs=[vmem, vmem, pl.BlockSpec(memory_space=pl.ANY)],
        out_specs=(vmem, vmem),
        scratch_shapes=[
            VMEM((n, msg_rows, 128), F32), VMEM((KX * 8 * BLK, 128), F32),
            VMEM(plane, F32), VMEM((2, UROWS, 128), F32), VMEM(plane, F32),
            VMEM((7,) + plane, F32), VMEM((4,) + plane, F32),
            VMEM((3, 2, 2, 8, 128), F32), VMEM((3, 2, 2, 8, 128), F32),
            VMEM((3, 2, 16, 128), F32), VMEM((3, 2, 16, 128), F32),
            VMEM((2, 2, 8, 128), F32), VMEM((2, n, 8, 128), F32), VMEM((2, ng, 8, 128), F32),
            dma, dma((n,)), dma((n,)), dma((3, 2)), dma((3, 2)), dma((3, 2)), dma((3, 2)),
            dma((2, n)), dma((2, n)), dma((2, ng)), dma((2, ng)),
        ],
        compiler_params=pltpu.CompilerParams(collective_id=1, has_side_effects=True, vmem_limit_bytes=big),
        name="barotropic",
    )(table, grid_depth, msg)
    return heat_new, salt_new, height, misfit


def solution(mesh):
    n, ng = mesh.shape["gx"], mesh.shape["gy"]
    slots = P(("gx", "gy"), None)
    cube = P(("gx", "gy"), None, None)
    grid = P("gy", "gx")
    return jax.shard_map(
        functools.partial(on_device, n, ng),
        mesh=mesh,
        in_specs=(cube, cube, slots, P(), P(("gx", "gy")), slots, grid),
        out_specs=(cube, cube, grid, grid),
        check_vma=False,
    )
```

```python
import functools

import jax
import jax.numpy as jnp
from jax import lax
from jax.experimental import pallas as pl
from jax.experimental.pallas import tpu as pltpu
from jax.sharding import PartitionSpec as P

SPAN_E = 60
SPAN_N = 50
KX = 3
KY = 6
LEVELS = 30
SLOTS = KX * KY
CELLS = SPAN_E * SPAN_N
ROWS = KY * SPAN_N
COLS = KX * SPAN_E
TILES = 24
HALINE = 0.8
THERMAL = 0.6
DAMPING = 0.05

BIG = 56 * 2**20
TOP = 16
PLANE = 328
UROWS = TOP + SPAN_N * 8
BLK = 32
EAST = COLS - 128
MESH = pl.DeviceIdType.MESH
F32 = jnp.float32
I32 = jnp.int32
VMEM = pltpu.VMEM


def iota(shape, dim):
    return lax.broadcasted_iota(I32, shape, dim)


def lroll(x, shift):
    shift = shift % x.shape[1]
    return x if shift == 0 else pltpu.roll(x, shift, 1)


def sroll(x, shift):
    shift = shift % x.shape[0]
    return x if shift == 0 else pltpu.roll(x, shift, 0)


def lreverse(x):
    lane = iota(x.shape, 1)
    bit = 1
    while bit < 128:
        x = jnp.where((lane & bit) != 0, lroll(x, bit), lroll(x, -bit))
        bit *= 2
    return x


def flip_cols(a, b):
    ra, rb = lreverse(b), lreverse(a)
    shift = 256 - COLS
    lane = iota(a.shape, 1)
    xa, xb = lroll(ra, -shift), lroll(rb, -shift)
    return jnp.where(lane < 128 - shift, xa, xb), jnp.where(lane < 128 - shift, xb, xa)


def message_rows(cap):
    return cap * TILES + (cap * 3 + 7) // 8 * 8


def greet(peers):
    sem = pltpu.get_barrier_semaphore()
    for peer in peers:
        pl.semaphore_signal(sem, inc=1, device_id=peer, device_id_type=MESH)
    return lambda: pl.semaphore_wait(sem, len(peers))


class Exchange:
    def __init__(self, n, ng, g, y, row_out, row_in, col_out, col_in, row_s, row_r, col_s, col_r):
        self.n, self.ng, self.g, self.y = n, ng, g, y
        self.row_out, self.row_in, self.col_out, self.col_in = row_out, row_in, col_out, col_in
        self.row_s, self.row_r, self.col_s, self.col_r = row_s, row_r, col_s, col_r

    def start_rows(self, k, north, north_folded, south):
        n, ng, g, y = self.n, self.ng, self.g, self.y
        top = lax.div(y + 1, ng)
        flipped = flip_cols(*north_folded)
        for half in range(2):
            self.row_out[k, 0, half] = jnp.where(y == ng - 1, flipped[half], north[half])
            self.row_out[k, 1, half] = south[half]
        up = pltpu.make_async_remote_copy(
            self.row_out.at[k, 0], self.row_in.at[k, top], self.row_s.at[k, 0], self.row_r.at[k, top],
            device_id=(g + top * (n - 1 - 2 * g), y + 1 - top), device_id_type=MESH,
        )
        down = pltpu.make_async_remote_copy(
            self.row_out.at[k, 1], self.row_in.at[k, 1], self.row_s.at[k, 1], self.row_r.at[k, 1],
            device_id=(g, lax.rem(y + ng - 1, ng)), device_id_type=MESH,
        )
        up.start()

        @pl.when(y > 0)
        def _():
            down.start()

        return up, down

    def wait_rows(self, k, up, down):
        g, y, ng = self.g, self.y, self.ng
        up.wait_send()

        @pl.when(y > 0)
        def _():
            down.wait_send()
            south = pltpu.make_async_remote_copy(
                self.row_out.at[k, 1], self.row_in.at[k, 0], self.row_s.at[k, 1], self.row_r.at[k, 0],
                device_id=(g, lax.rem(y + ng - 1, ng)), device_id_type=MESH,
            )
            south.wait_recv()

        down.wait_recv()

        @pl.when(y == 0)
        def _():
            self.row_in[k, 0] = jnp.zeros((2, 8, 128), F32)

        return [self.row_in[k, 0, half] for half in range(2)], [self.row_in[k, 1, half] for half in range(2)]

    def start_cols(self, k):
        n, g, y = self.n, self.g, self.y
        copies = []
        for slot, target in ((0, lax.rem(g + 1, n)), (1, lax.rem(g + n - 1, n))):
            copy = pltpu.make_async_remote_copy(
                self.col_out.at[k, slot], self.col_in.at[k, slot], self.col_s.at[k, slot], self.col_r.at[k, slot],
                device_id=(target, y), device_id_type=MESH,
            )
            copy.start()
            copies.append(copy)
        return copies


    def halo_rows(self, k, plane):
        sub = iota((8, 128), 0)
        north = [plane[half, 312:320, :] for half in range(2)]
        south = [plane[half, 16:24, :] for half in range(2)]
        turned = [
            jnp.where(
                sub < 2,
                jnp.where(sub == 0, sroll(v, -3), sroll(v, -1)),
                jnp.where(sub == 2, sroll(v, 1), sroll(v, 3)),
            )
            for v in north
        ]
        return self.start_rows(k, north, turned, south)

    def halo_cols(self, k, plane, rows):
        sub = iota((8, 128), 0)
        lane = iota((8, 128), 1)
        below, above = self.wait_rows(k, *rows)
        for half in range(2):
            plane[half, 8:16, :] = sroll(below[half], 4)
            plane[half, 312:320, :] = jnp.where(sub < 4, plane[half, 312:320, :], sroll(above[half], 4))
        for part in range(2):
            to_east = jnp.zeros((8, 128), F32)
            to_west = jnp.zeros((8, 128), F32)
            for t in range(32 * part, min(39, 32 * part + 32)):
                first = 4 * (t - 32 * part)
                here = (lane >= first) & (lane < first + 4)
                rows = slice(8 + 8 * t, 16 + 8 * t)
                to_east = jnp.where(here, lroll(plane[1, rows, :], first - (EAST - 4)), to_east)
                to_west = jnp.where(here, lroll(plane[0, rows, :], first), to_west)
            self.col_out[k, 0, 8 * part : 8 * part + 8, :] = to_east
            self.col_out[k, 1, 8 * part : 8 * part + 8, :] = to_west
        return self.start_cols(k)

    def halo_end(self, k, plane, copies):
        lane = iota((8, 128), 1)
        for copy in copies:
            copy.wait()
        for part in range(2):
            west = self.col_in[k, 0, 8 * part : 8 * part + 8, :]
            east = self.col_in[k, 1, 8 * part : 8 * part + 8, :]
            for t in range(32 * part, min(39, 32 * part + 32)):
                first = 4 * (t - 32 * part)
                rows = slice(8 + 8 * t, 16 + 8 * t)
                plane[1, rows, :] = jnp.where(
                    lane >= 124,
                    lroll(west, 124 - first),
                    jnp.where((lane >= EAST) & (lane < EAST + 4), lroll(east, EAST - first), plane[1, rows, :]),
                )

    def halo(self, k, plane):
        self.halo_end(k, plane, self.halo_cols(k, plane, self.halo_rows(k, plane)))


STRIP_ROWS = 48
NEAR = 40


def strips_kernel(n, ng, cap, ids_ref, dfac_ref, depth_hbm, slot_hbm, flux_hbm,
                  all_ref, tab_ref, dpl, coef, nflat, fflat,
                  depth_ref, slot_ref, flux_ref, pa, pb, msg, edge, got,
                  row_out, row_in, col_out, col_in,
                  own, s1, r1, s2, r2, s3, r3, row_s, row_r, col_s, col_r):
    g = lax.axis_index("gx")
    y = lax.axis_index("gy")
    loads = [
        pltpu.make_async_copy(src, dst, own.at[k])
        for k, (src, dst) in enumerate(((depth_hbm, depth_ref), (slot_hbm, slot_ref), (flux_hbm, flux_ref)))
    ]
    for load in loads:
        load.start()
    up, down = lax.rem(y + 1, ng), lax.rem(y + ng - 1, ng)
    band = [(lax.rem(g + k, n), y) for k in range(1, n)]
    everyone = greet(band + [(g, up), (g, down)])
    exchange = Exchange(n, ng, g, y, row_out, row_in, col_out, col_in, row_s, row_r, col_s, col_r)
    lane = iota((8, 128), 1)
    row = iota((1, 128), 1)
    code = jnp.full((1, 128), -1, I32)
    owners = []
    for s in range(SLOTS):
        block = jnp.maximum(ids_ref[s], 0)
        bx = lax.rem(block, KX * n)
        by = lax.rem(lax.div(block, KX * n), KY)
        owner = jnp.where(ids_ref[s] >= 0, lax.div(bx, KX), -1)
        rank = jnp.int32(0)
        for other in owners:
            rank = rank + jnp.where(other == owner, 1, 0)
        owners.append(owner)
        value = (owner * 32 + by * KX + lax.rem(bx, KX)) * 32 + rank
        code = jnp.where(row == s, jnp.where(owner >= 0, value, -1), code)
    loads[0].wait()
    pa[0:ROWS, :] = depth_ref[:, 0:128]
    pb[0:ROWS, 0:EAST] = depth_ref[:, 128:COLS]
    rims = [jnp.zeros((8, 128), I32) for _ in range(KX)]
    ns = []
    for i in range(SPAN_N):
        off = SPAN_E * i % 128
        a = pa[pl.ds(i, 8, stride=SPAN_N), :]
        b = pb[pl.ds(i, 8, stride=SPAN_N), :]
        cells = [a, a, jnp.where(lane < 64, b, a)]
        push = 0 if i < 32 else 1
        first, last = (off + push) % 128, (off + SPAN_E - 1 - push) % 128
        for bx in range(KX):
            turn = off - SPAN_E * bx
            rims[bx] = jnp.where(lane == first, lroll(cells[bx], turn + push), rims[bx])
            rims[bx] = jnp.where(lane == last, lroll(cells[bx], turn - push), rims[bx])
        if i == 0:
            ns = [lroll(cells[bx], -SPAN_E * bx) for bx in range(KX)]
        if i == SPAN_N - 1:
            ns = [
                jnp.where(lane < SPAN_E, ns[bx], lroll(cells[bx], SPAN_E - SPAN_E * bx))
                for bx in range(KX)
            ]
    for bx in range(KX):
        for part, value in enumerate((rims[bx], ns[bx])):
            msg[pl.ds(bx * 2 + part, 8, stride=6), :] = value
    msg[36:37, :] = code
    edge[...] = jnp.zeros((8, 128), I32)
    for bx in range(KX):
        edge[bx : bx + 1, :] = ns[bx][0:1]
        edge[3 + bx : 4 + bx, :] = ns[bx][KY - 1 : KY]
    zero8 = jnp.zeros((8, 128), F32)
    for half in range(2):
        dpl[half, 0:16, :] = jnp.zeros((16, 128), F32)
        dpl[half, 312:PLANE, :] = jnp.zeros((PLANE - 312, 128), F32)
    dpl[0, TOP : TOP + ROWS, :] = depth_ref[:, 0:128].astype(F32)
    dpl[1, TOP : TOP + ROWS, :] = jnp.zeros((ROWS, 128), F32)
    dpl[1, TOP : TOP + ROWS, 0:EAST] = depth_ref[:, 128:COLS].astype(F32)

    everyone()
    copies = []
    for slot, target in ((0, up), (1, down)):
        copy = pltpu.make_async_remote_copy(
            edge, got.at[slot], s1.at[slot], r1.at[slot], device_id=(g, target), device_id_type=MESH
        )
        copy.start()
        copies.append(copy)
    rows = exchange.halo_rows(0, dpl)
    sends = []
    for k, peer in enumerate(band):
        copy = pltpu.make_async_remote_copy(
            msg.at[pl.ds(0, NEAR)], all_ref.at[g, pl.ds(0, NEAR)], s2.at[k], r2.at[k],
            device_id=peer, device_id_type=MESH,
        )
        copy.start()
        sends.append(copy)
    gain = jnp.zeros((1, 128), F32)
    for k in range(LEVELS):
        above = dfac_ref[k - 1] if k > 0 else jnp.float32(0)
        below = dfac_ref[k] if k + 1 < LEVELS else jnp.float32(0)
        base = (1.0 + above) - above * gain
        full = 1.0 / (base + below)
        gain = below * full
        coef[0, k : k + 1, :] = full
        coef[1, k : k + 1, :] = 1.0 / base
        coef[2, k : k + 1, :] = jnp.broadcast_to(above, (1, 128))
        coef[3, k : k + 1, :] = gain
    for copy in copies:
        copy.wait()
    near = edge
    for bx in range(KX):
        mirrored = lroll(lreverse(ns[bx]), -8)[KY - 1 : KY]
        near[bx : bx + 1, :] = jnp.where(y == ng - 1, mirrored, got[1, bx : bx + 1, :])
        near[3 + bx : 4 + bx, :] = got[0, 3 + bx : 4 + bx, :]
    for k, peer in enumerate(band):
        copy = pltpu.make_async_remote_copy(
            near, all_ref.at[g, pl.ds(NEAR, 8)], s3.at[k], r3.at[k], device_id=peer, device_id_type=MESH
        )
        copy.start()
        sends.append(copy)
    cols = exchange.halo_cols(0, dpl, rows)
    all_ref[pl.ds(g, 1), 0:NEAR] = msg[0:NEAR, :][None]
    all_ref[pl.ds(g, 1), NEAR:STRIP_ROWS] = near[...][None]
    loads[1].wait()
    loads[2].wait()
    for t in range(TILES):
        width = min(128, CELLS - 128 * t)
        span = slice(t * 128, t * 128 + width)
        for first in (0, 8, 16):
            number = min(8, SLOTS - first)
            place = pl.ds(first * TILES + t, number, stride=TILES)
            for src, dst, kind in ((slot_ref, nflat, I32), (flux_ref, fflat, F32)):
                value = src[first : first + number, span]
                if width < 128:
                    value = jnp.concatenate([value, jnp.zeros((number, 128 - width), kind)], axis=1)
                dst[place, :] = value
    exchange.halo_end(0, dpl, cols)
    for copy in sends:
        copy.wait()
    codes = all_ref[:, 36, :]
    key = codes >> 5
    rank = codes & 31
    source = iota((n, 128), 0)
    number = (source * cap + rank + 1).astype(F32)
    for p in range(SLOTS):
        hit = jnp.where(key == g * 32 + p, number, 0.0)
        hit = jnp.sum(jnp.sum(hit, axis=0, keepdims=True), axis=1, keepdims=True)
        tab_ref[p : p + 1, :] = jnp.broadcast_to(hit.astype(I32) - 1, (1, 128))
    tab_ref[SLOTS:24, :] = jnp.full((24 - SLOTS, 128), -1, I32)


def ahead(x, step):
    a = lroll(x, -step)
    return jnp.where(iota(x.shape, 1) < 128 - step, a, sroll(a, -1))


def behind(x, step):
    a = lroll(x, step)
    return jnp.where(iota(x.shape, 1) >= step, a, sroll(a, 1))


STEP = 33
AHEAD = 5


def columns_kernel(n, ng, cap, ids_ref, coef, fflat, nflat, strips_ref, heat_hbm, salt_hbm,
                   heat_out, salt_out, msg_ref, heat_in, salt_in, jcol, inh, ins, yh, ys, oh, os_, count, sems):
    step = pl.program_id(0)
    shape = (TILES, 128)
    row24 = iota(shape, 0)
    lane24 = iota(shape, 1)
    cell = row24 * 128 + lane24
    lane = iota((1, 128), 1)
    last = CELLS - 128 * (TILES - 1)

    ring = AHEAD + 1

    def loads(slot):
        place = lax.rem(slot, ring)
        return [
            pltpu.make_async_copy(src.at[slot], dst.at[place], sems.at[place, which])
            for which, (src, dst) in enumerate(((heat_hbm, heat_in), (salt_hbm, salt_in)))
        ]

    @pl.when(step == 0)
    def _():
        for slot in range(AHEAD):
            for load in loads(slot):
                load.start()
        flat = cell.astype(F32)
        whole = jnp.floor((flat + 0.5) * (1.0 / SPAN_E))
        jcol[...] = cell - whole.astype(I32) * SPAN_E
        for d in range(n):
            count[d] = 0

    @pl.when(step + AHEAD < SLOTS)
    def _():
        for load in loads(step + AHEAD):
            load.start()

    for load in loads(step):
        load.wait()
    here = lax.rem(step, ring)
    for t in range(TILES):
        width = 128 if t < TILES - 1 else last
        cols = slice(t * 128, t * 128 + width)
        inh[t * STEP : t * STEP + LEVELS, 0:width] = heat_in[here, :, cols]
        ins[t * STEP : t * STEP + LEVELS, 0:width] = salt_in[here, :, cols]

    mine = pl.ds(pl.multiple_of(step * TILES, 8), TILES)
    depth = nflat[mine, :]
    wet = depth > 0
    h = s = None
    for k in range(LEVELS):
        level = pl.ds(k, TILES, stride=STEP)
        rh = inh[level, :]
        rs = ins[level, :]
        deeper = depth > k + 1
        if k == 0:
            rh = rh + jnp.where(wet, fflat[mine, :], 0.0)
            pivot = jnp.where(deeper, coef[0, 0:1, :], 1.0)
            h = rh * pivot
            s = rs * pivot
        else:
            above = jnp.where(wet, coef[2, k : k + 1, :], 0.0)
            pivot = jnp.where(wet, coef[1, k : k + 1, :], 1.0)
            if k + 1 < LEVELS:
                pivot = jnp.where(deeper, coef[0, k : k + 1, :], pivot)
            h = (rh + above * h) * pivot
            s = (rs + above * s) * pivot
        if k + 1 < LEVELS:
            yh[k * TILES : (k + 1) * TILES, :] = h
            ys[k * TILES : (k + 1) * TILES, :] = s
        wet = deeper
    level = pl.ds(LEVELS - 1, TILES, stride=STEP)
    oh[level, :] = h
    os_[level, :] = s
    for k in range(LEVELS - 2, -1, -1):
        gain = jnp.where(depth > k + 1, coef[3, k : k + 1, :], 0.0)
        h = yh[k * TILES : (k + 1) * TILES, :] + gain * h
        s = ys[k * TILES : (k + 1) * TILES, :] + gain * s
        level = pl.ds(k, TILES, stride=STEP)
        oh[level, :] = h
        os_[level, :] = s
    for t in range(TILES):
        width = 128 if t < TILES - 1 else last
        cols = slice(t * 128, t * 128 + width)
        heat_out[0, :, cols] = oh[t * STEP : t * STEP + LEVELS, 0:width]
        salt_out[0, :, cols] = os_[t * STEP : t * STEP + LEVELS, 0:width]

    blocks_x = KX * n
    ident = ids_ref[step]
    block = jnp.maximum(ident, 0)
    bx = lax.rem(block, blocks_x)
    by = lax.div(block, blocks_x)
    byl = lax.rem(by, KY)
    dev = lax.div(bx, KX)
    bxl = lax.rem(bx, KX)

    def strip(device, place):
        return strips_ref[device, pl.ds(place, 1), :]

    def rim_of(col):
        return strip(lax.div(col, KX), (byl * KX + lax.rem(col, KX)) * 2)

    east = rim_of(lax.rem(bx + 1, blocks_x))
    west = rim_of(lax.rem(bx + blocks_x - 1, blocks_x))
    ew = [
        jnp.where((lane & 3) == 3, lroll(east, SPAN_E - 1 - push), lroll(west, 1 - SPAN_E + push))
        for push in range(2)
    ]
    ew = jnp.where(row24 < 15, ew[0], ew[1])
    mirror = blocks_x - 1 - bx
    mirrored = lax.rem(mirror, KX)
    folded = by == KY * ng - 1
    inner = byl < KY - 1
    north_dev = jnp.where(folded, lax.div(mirror, KX), dev)
    north_row = jnp.where(
        inner,
        ((byl + 1) * KX + bxl) * 2 + 1,
        jnp.where(folded, NEAR + mirrored, NEAR + bxl),
    )
    north = lroll(strip(north_dev, north_row), -4)
    south_row = jnp.where(byl > 0, ((byl - 1) * KX + bxl) * 2 + 1, NEAR + 3 + bxl)
    south = jnp.where(by > 0, lroll(strip(dev, south_row), -SPAN_E), 0)
    j = jcol[...]
    inside = cell < CELLS
    first_j = j == 0
    last_j = j == SPAN_E - 1
    first_i = cell < SPAN_E
    last_i = cell >= CELLS - SPAN_E
    faces = (
        jnp.minimum(depth, jnp.where(last_j, ew, ahead(depth, 1))),
        jnp.minimum(depth, jnp.where(first_j, ew, behind(depth, 1))),
        jnp.minimum(depth, jnp.where(last_i, north, ahead(depth, SPAN_E))),
        jnp.minimum(depth, jnp.where(first_i, south, behind(depth, SPAN_E))),
    )
    sums = [jnp.zeros(shape, F32) for _ in range(4)]
    pressure = jnp.zeros(shape, F32)
    total = jnp.zeros(shape, F32)
    for k in range(LEVELS):
        level = pl.ds(k, TILES, stride=STEP)
        pressure = pressure + (HALINE * os_[level, :] - THERMAL * oh[level, :])
        total = total + pressure
        sums = [jnp.where(face == k + 1, total, held) for face, held in zip(faces, sums)]
    sums = [jnp.where(inside, held, 0.0) for held in sums]
    se, sw, sn, ss = sums
    local = jnp.where(last_j, 0.0, ahead(sw, 1)) - se
    local = local + (jnp.where(first_j, 0.0, behind(se, 1)) - sw)
    local = local + (jnp.where(last_i, 0.0, ahead(ss, SPAN_E)) - sn)
    local = local + (jnp.where(first_i, 0.0, behind(sn, SPAN_E)) - ss)
    local = jnp.where(inside, local, 0.0)
    rim = jnp.where(last_j, se, jnp.where(first_j, sw, 0.0))
    rim0 = jnp.sum(jnp.where(row24 < 15, rim, 0.0), axis=0, keepdims=True)
    rim1 = jnp.sum(jnp.where(row24 >= 15, rim, 0.0), axis=0, keepdims=True)
    top = jnp.sum(jnp.where(last_i, sn, 0.0), axis=0, keepdims=True)
    bottom = jnp.sum(jnp.where(first_i, ss, 0.0), axis=0, keepdims=True)
    cap_row = jnp.where(lane < SPAN_E, bottom, jnp.where(lane < 2 * SPAN_E, lroll(top, 64), 0.0))

    @pl.when(ident >= 0)
    def _():
        rank = count[dev]
        count[dev] = rank + 1
        msg_ref[dev, pl.ds(pl.multiple_of(rank * TILES, 8), TILES), :] = local
        base = cap * TILES + rank * 3
        for part, value in enumerate((rim0, rim1, cap_row)):
            msg_ref[dev, pl.ds(base + part, 1), :] = value


def barotropic_kernel(n, ng, cap, tab_ref, dpl, msg_ref, height_ref, misfit_ref,
                      recv, blk, upl, zpl, wts, qpl, row_out, row_in, col_out, col_in,
                      red_out, red_x, red_y, own_sem, a2a_s, a2a_r, row_s, row_r, col_s, col_r,
                      rx_s, rx_r, ry_s, ry_r):
    g = lax.axis_index("gx")
    y = lax.axis_index("gy")
    band = [(lax.rem(g + k, n), y) for k in range(1, n)]
    column = [(g, lax.rem(y + k, ng)) for k in range(1, ng)]
    everyone = greet(band + column)
    exchange = Exchange(n, ng, g, y, row_out, row_in, col_out, col_in, row_s, row_r, col_s, col_r)
    lane = iota((8, 128), 1)
    sub = iota((8, 128), 0)
    zero8 = jnp.zeros((8, 128), F32)
    for half in range(2):
        for ref in (zpl, qpl.at[0], qpl.at[1], qpl.at[2], qpl.at[3]):
            ref[half, 0:8, :] = zero8
            ref[half, 320:PLANE, :] = zero8

    span = 24
    chunks = 13
    lane_c = iota((span, 128), 1)

    def rows_at(t, shift=0):
        return pl.ds(8 + t * span + shift, span)

    def both(ref, rows):
        return [ref[half, rows, :] for half in range(2)]

    def from_east(pair):
        a, b = [lroll(v, -1) for v in pair]
        return jnp.where(lane_c < 127, a, b), jnp.where(lane_c < 127, b, a)

    def from_west(pair):
        a, b = [lroll(v, 1) for v in pair]
        return jnp.where(lane_c >= 1, a, b), jnp.where(lane_c >= 1, b, a)

    def weigh(t, carry):
        rows = rows_at(t)
        d = both(dpl, rows)
        beside = (from_east(d), from_west(d), both(dpl, rows_at(t, 1)), both(dpl, rows_at(t, -1)))
        r = iota((span, 128), 0) + (8 + t * span)
        for half in range(2):
            damp = jnp.where(d[half] > 0, DAMPING, 1.0)
            diagonal = damp
            for side in range(4):
                w = jnp.minimum(d[half], beside[side][half]) * (1.0 / LEVELS)
                wts[side, half, rows, :] = w
                diagonal = diagonal + w
            inverse = 1.0 / diagonal
            wts[4, half, rows, :] = damp
            wts[5, half, rows, :] = inverse
            inside = (r >= TOP) & (r < TOP + ROWS)
            if half == 1:
                inside = inside & (lane_c < EAST)
            wts[6, half, rows, :] = jnp.where(inside, inverse, 0.0)
        return carry

    lax.fori_loop(0, chunks, weigh, 0)

    everyone()
    own = pltpu.make_async_copy(msg_ref.at[g], recv.at[g], own_sem)
    own.start()
    sends = []
    for k, peer in enumerate(band):
        copy = pltpu.make_async_remote_copy(
            msg_ref.at[peer[0]], recv.at[g], a2a_s.at[k], a2a_r.at[k], device_id=peer, device_id_type=MESH
        )
        copy.start()
        sends.append(copy)


    own.wait()
    for copy in sends:
        copy.wait()
    for bx in range(KX):
        blk[(bx * 8 + KY) * BLK : (bx + 1) * 8 * BLK, :] = jnp.zeros((2 * BLK, 128), F32)
        wanted = [
            jnp.broadcast_to(tab_ref[by * KX + bx : by * KX + bx + 1, :], (8, 128)) for by in range(KY)
        ]

        def pick(source, held, wanted=wanted):
            held = list(held)
            for rank in range(cap):
                parts = [recv[source, rank * TILES + 8 * v : rank * TILES + 8 * v + 8, :] for v in range(3)]
                first = cap * TILES + rank * 3
                rest = recv[source, first : first + 3, :]
                for by in range(KY):
                    hit = wanted[by] == source * cap + rank
                    for v in range(3):
                        held[by * 4 + v] = jnp.where(hit, parts[v], held[by * 4 + v])
                    held[by * 4 + 3] = jnp.where(hit[0:3], rest, held[by * 4 + 3])
            return tuple(held)

        start = ([zero8] * 3 + [jnp.zeros((3, 128), F32)]) * KY
        held = lax.fori_loop(0, n, pick, tuple(start))
        for by in range(KY):
            base = (bx * 8 + by) * BLK
            for v in range(3):
                blk[base + 8 * v : base + 8 * v + 8, :] = held[by * 4 + v]
            blk[base + TILES : base + TILES + 3, :] = held[by * 4 + 3]

    def rows_of(bx, row):
        return blk[pl.ds(bx * 8 * BLK + row, 8, stride=BLK), :]

    rims = [[rows_of(bx, TILES + part) for part in range(2)] for bx in range(KX)]
    for part in range(2):
        col_out[0, 0, 8 * part : 8 * part + 8, :] = rims[KX - 1][part]
        col_out[0, 1, 8 * part : 8 * part + 8, :] = rims[0][part]
    cap_rows = [rows_of(bx, TILES + 2) for bx in range(KX)]

    def lay(v):
        tail = jnp.where(lane < EAST, v[2], 0.0)
        return jnp.where(lane < 60, v[0], jnp.where(lane < 120, v[1], v[2])), tail

    souths = lay([lroll(cap_rows[bx], SPAN_E * bx) for bx in range(KX)])
    norths = lay([lroll(cap_rows[bx], SPAN_E * bx - SPAN_E) for bx in range(KX)])
    waits = exchange.start_rows(0, norths, [sroll(v, 8 - (KY - 1)) for v in norths], souths)
    col_copies = exchange.start_cols(0)
    for i in range(SPAN_N):
        t, off = SPAN_E * i // 128, SPAN_E * i % 128
        cells = []
        for bx in range(KX):
            value = rows_of(bx, t)
            if off + SPAN_E > 128:
                value = jnp.where(lane >= off, value, rows_of(bx, t + 1))
            cells.append(lroll(value, SPAN_E * bx - off))
        first, second = lay(cells)
        rim = [rims[bx][i // 32] for bx in range(KX)]
        first = first + jnp.where(
            lane == 59,
            lroll(rim[1], 59 - off),
            jnp.where(
                lane == 60,
                lroll(rim[0], 1 - off),
                jnp.where(lane == 119, lroll(rim[2], 119 - off), jnp.where(lane == 120, lroll(rim[1], 61 - off), 0.0)),
            ),
        )
        if i == SPAN_N - 1:
            first = first + jnp.where(sub < KY - 1, sroll(souths[0], -1), 0.0)
            second = second + jnp.where(sub < KY - 1, sroll(souths[1], -1), 0.0)
        if i == 0:
            first = first + jnp.where((sub > 0) & (sub < KY), sroll(norths[0], 1), 0.0)
            second = second + jnp.where((sub > 0) & (sub < KY), sroll(norths[1], 1), 0.0)
        upl[0, pl.ds(TOP + i, 8, stride=SPAN_N), :] = first
        upl[1, pl.ds(TOP + i, 8, stride=SPAN_N), :] = second
    below, above = exchange.wait_rows(0, *waits)
    for copy in col_copies:
        copy.wait()
    for half in range(2):
        upl[half, TOP : TOP + 1, :] = upl[half, TOP : TOP + 1, :] + below[half][KY - 1 : KY]
        end = TOP + ROWS - 1
        upl[half, end : end + 1, :] = upl[half, end : end + 1, :] + above[half][0:1]
        upl[half, 8:16, :] = zero8
    for i in range(SPAN_N):
        off = SPAN_E * i % 128
        part = slice(8 * (i // 32), 8 * (i // 32) + 8)
        rows = pl.ds(TOP + i, 8, stride=SPAN_N)
        west = lroll(col_in[0, 0, part, :], 1 - SPAN_E - off)
        east = lroll(col_in[0, 1, part, :], COLS - 1 - off)
        good = sub < KY
        upl[0, rows, :] = upl[0, rows, :] + jnp.where((lane == 0) & good, west, 0.0)
        upl[1, rows, :] = upl[1, rows, :] + jnp.where((lane == EAST - 1) & good, east, 0.0)

    def begin(t, carry):
        rows = rows_at(t)
        for half in range(2):
            rhs = upl[half, rows, :] * (1.0 / LEVELS)
            qpl[0, half, rows, :] = rhs
            zpl[half, rows, :] = rhs * wts[5, half, rows, :]
        return carry

    lax.fori_loop(0, chunks, begin, 0)
    exchange.halo(1, zpl)

    def image(out, scale_next):
        def body(t, carry):
            rows = rows_at(t)
            v = both(zpl, rows)
            beside = (from_east(v), from_west(v), both(zpl, rows_at(t, 1)), both(zpl, rows_at(t, -1)))
            for half in range(2):
                result = wts[4, half, rows, :] * v[half]
                for side in range(4):
                    result = result + wts[side, half, rows, :] * (v[half] - beside[side][half])
                qpl[out, half, rows, :] = result
            return carry

        lax.fori_loop(0, chunks, body, 0)
        if scale_next:

            def scale(t, carry):
                rows = rows_at(t)
                for half in range(2):
                    zpl[half, rows, :] = qpl[out, half, rows, :] * wts[5, half, rows, :]
                return carry

            lax.fori_loop(0, chunks, scale, 0)

    def everywhere(k, parts):
        red_out[k, 0] = zero8
        for place, part in enumerate(parts):
            red_out[k, 0, place : place + 1, :] = jnp.sum(part, axis=0, keepdims=True)
        for level, (peers, into, sem_s, sem_r, me) in enumerate(
            ((band, red_x, rx_s, rx_r, g), (column, red_y, ry_s, ry_r, y))
        ):
            copies = []
            for number, peer in enumerate(peers):
                copy = pltpu.make_async_remote_copy(
                    red_out.at[k, level], into.at[k, me], sem_s.at[k, number], sem_r.at[k, number],
                    device_id=peer, device_id_type=MESH,
                )
                copy.start()
                copies.append(copy)
            into[k, pl.ds(me, 1)] = red_out[k, level][None]
            for copy in copies:
                copy.wait()
            total = jnp.sum(into[k], axis=0)
            if level == 0:
                red_out[k, 1] = total
        total = jnp.sum(total, axis=1, keepdims=True)
        return [jnp.broadcast_to(total[place : place + 1], (8, 128)) for place in range(len(parts))]

    image(1, True)

    def first_dots(t, carry):
        rows = rows_at(t)
        a, b = carry
        for half in range(2):
            z = qpl[0, half, rows, :] * wts[6, half, rows, :]
            a = a + qpl[0, half, rows, :] * z
            b = b + qpl[1, half, rows, :] * z
        return a, b

    zero_c = jnp.zeros((span, 128), F32)
    mu = everywhere(0, lax.fori_loop(0, chunks, first_dots, (zero_c, zero_c)))
    image(2, True)
    image(3, False)
    norm = mu[0]
    ray = mu[1] / norm
    ray_c = jnp.broadcast_to(ray[0:1], (span, 128))

    def shift(t, carry):
        rows = rows_at(t)
        c = list(carry)
        for half in range(2):
            w0, w1, w2, w3 = [qpl[j, half, rows, :] for j in range(4)]
            q1 = w1 - ray_c * w0
            t2 = w2 - ray_c * w1
            t3 = (w3 - ray_c * w2) - ray_c * t2
            q2 = t2 - ray_c * q1
            q3 = t3 - ray_c * q2
            qpl[1, half, rows, :] = q1
            qpl[2, half, rows, :] = q2
            qpl[3, half, rows, :] = q3
            inverse = wts[6, half, rows, :]
            z1 = q1 * inverse
            z2 = q2 * inverse
            c[0] = c[0] + w0 * z1
            c[1] = c[1] + q1 * z1
            c[2] = c[2] + q2 * z1
            c[3] = c[3] + q2 * z2
            c[4] = c[4] + q3 * z2
        return tuple(c)

    moment = everywhere(1, lax.fori_loop(0, chunks, shift, (zero_c,) * 5))
    one = jnp.ones((8, 128), F32)
    scale = one / norm
    c = [one] + [m * scale for m in moment]
    zero = zero8
    rho = [one, zero, zero, zero]
    pi = [one, zero, zero]
    xs = [zero, zero, zero]
    gamma = one
    for it in range(3):
        curve = zero
        for i in range(it + 1):
            for j in range(it + 1):
                curve = curve + (pi[i] * pi[j]) * (ray * c[i + j] + c[i + j + 1])
        alpha = gamma / curve
        xs = [xs[i] + alpha * pi[i] if i <= it else xs[i] for i in range(3)]
        for i in range(it + 2):
            step = ray * pi[i] if i <= it else zero
            if i > 0:
                step = step + pi[i - 1]
            rho[i] = rho[i] - alpha * step
        if it == 2:
            break
        gamma_new = zero
        for i in range(it + 2):
            for j in range(it + 2):
                gamma_new = gamma_new + (rho[i] * rho[j]) * c[i + j]
        beta = gamma_new / gamma
        pi = [rho[i] + beta * pi[i] for i in range(3)]
        gamma = gamma_new

    def finish(first, size):
        rows = pl.ds(TOP + first, size)
        out = pl.ds(first, size)
        x = [jnp.broadcast_to(v[0:1], (size, 128)) for v in xs]
        r = [jnp.broadcast_to(v[0:1], (size, 128)) for v in rho]
        for half in range(2):
            q = [qpl[j, half, rows, :] for j in range(4)]
            high = (x[0] * q[0] + x[1] * q[1] + x[2] * q[2]) * wts[5, half, rows, :]
            rest = r[0] * q[0] + r[1] * q[1] + r[2] * q[2] + r[3] * q[3]
            if half == 0:
                height_ref[out, 0:128] = high
                misfit_ref[out, 0:128] = rest
            else:
                height_ref[out, 128:COLS] = high[:, 0:EAST]
                misfit_ref[out, 128:COLS] = rest[:, 0:EAST]

    def finish_chunk(t, carry):
        finish(pl.multiple_of(t * span, 8), span)
        return carry

    lax.fori_loop(0, ROWS // span, finish_chunk, 0)
    finish(ROWS // span * span, ROWS % span)


def strips_call(n, ng, flux, dfac, ids, slot_depth, grid_depth):
    vmem = pl.BlockSpec(memory_space=VMEM)
    smem = pl.BlockSpec(memory_space=pltpu.SMEM)
    hbm = pl.BlockSpec(memory_space=pl.ANY)
    dma = pltpu.SemaphoreType.DMA
    flat = (SLOTS * TILES, 128)
    return pl.pallas_call(
        functools.partial(strips_kernel, n, ng, (SLOTS + n - 1) // n),
        out_shape=(
            jax.ShapeDtypeStruct((n, STRIP_ROWS, 128), I32), jax.ShapeDtypeStruct((24, 128), I32),
            jax.ShapeDtypeStruct((2, PLANE, 128), F32), jax.ShapeDtypeStruct((4, 32, 128), F32),
            jax.ShapeDtypeStruct(flat, I32), jax.ShapeDtypeStruct(flat, F32),
        ),
        in_specs=[smem, smem, hbm, hbm, hbm],
        out_specs=(vmem,) * 6,
        scratch_shapes=[
            VMEM((ROWS, COLS), I32), VMEM((SLOTS, CELLS), I32), VMEM((SLOTS, CELLS), F32),
            VMEM((400, 128), I32), VMEM((400, 128), I32), VMEM((48, 128), I32), VMEM((8, 128), I32),
            VMEM((2, 8, 128), I32),
            VMEM((1, 2, 2, 8, 128), F32), VMEM((1, 2, 2, 8, 128), F32),
            VMEM((1, 2, 16, 128), F32), VMEM((1, 2, 16, 128), F32),
            dma((3,)), dma((2,)), dma((2,)), dma((n,)), dma((n,)), dma((n,)), dma((n,)),
            dma((1, 2)), dma((1, 2)), dma((1, 2)), dma((1, 2)),
        ],
        compiler_params=pltpu.CompilerParams(collective_id=0, has_side_effects=True, vmem_limit_bytes=BIG),
        name="strips",
    )(ids, dfac, grid_depth, slot_depth, flux)


def columns_call(n, ng, heat, salt, ids, coef, fflat, nflat, strips):
    cap = (SLOTS + n - 1) // n
    msg_rows = message_rows(cap)
    smem = pl.BlockSpec(memory_space=pltpu.SMEM)
    hbm = pl.BlockSpec(memory_space=pl.ANY)
    fixed = lambda shape: pl.BlockSpec(shape, lambda s: (0,) * len(shape))
    block = pl.BlockSpec((1, LEVELS, CELLS), lambda s: (s, 0, 0))
    ring = (AHEAD + 1, LEVELS, CELLS)
    tall = TILES * STEP + 8
    return pl.pallas_call(
        functools.partial(columns_kernel, n, ng, cap),
        grid=(SLOTS,),
        out_shape=(
            jax.ShapeDtypeStruct(heat.shape, F32),
            jax.ShapeDtypeStruct(salt.shape, F32),
            jax.ShapeDtypeStruct((n, msg_rows, 128), F32),
        ),
        in_specs=[
            smem, fixed((4, 32, 128)), fixed((SLOTS * TILES, 128)), fixed((SLOTS * TILES, 128)),
            fixed((n, STRIP_ROWS, 128)), hbm, hbm,
        ],
        out_specs=(block, block, fixed((n, msg_rows, 128))),
        scratch_shapes=[
            VMEM(ring, F32), VMEM(ring, F32), VMEM((TILES, 128), I32),
            VMEM((tall, 128), F32), VMEM((tall, 128), F32),
            VMEM((TILES * LEVELS, 128), F32), VMEM((TILES * LEVELS, 128), F32),
            VMEM((tall, 128), F32), VMEM((tall, 128), F32),
            pltpu.SMEM((n,), I32), pltpu.SemaphoreType.DMA((AHEAD + 1, 2)),
        ],
        compiler_params=pltpu.CompilerParams(vmem_limit_bytes=BIG),
        name="columns",
    )(ids, coef, fflat, nflat, strips, heat, salt)


def barotropic_call(n, ng, table, depths, msg):
    cap = (SLOTS + n - 1) // n
    vmem = pl.BlockSpec(memory_space=VMEM)
    dma = pltpu.SemaphoreType.DMA
    field = jax.ShapeDtypeStruct((ROWS, COLS), F32)
    plane = (2, PLANE, 128)
    return pl.pallas_call(
        functools.partial(barotropic_kernel, n, ng, cap),
        out_shape=(field, field),
        in_specs=[vmem, vmem, pl.BlockSpec(memory_space=pl.ANY)],
        out_specs=(vmem, vmem),
        scratch_shapes=[
            VMEM((n, message_rows(cap), 128), F32), VMEM((KX * 8 * BLK, 128), F32),
            VMEM((2, UROWS, 128), F32), VMEM(plane, F32),
            VMEM((7,) + plane, F32), VMEM((4,) + plane, F32),
            VMEM((2, 2, 2, 8, 128), F32), VMEM((2, 2, 2, 8, 128), F32),
            VMEM((2, 2, 16, 128), F32), VMEM((2, 2, 16, 128), F32),
            VMEM((2, 2, 8, 128), F32), VMEM((2, n, 8, 128), F32), VMEM((2, ng, 8, 128), F32),
            dma, dma((n,)), dma((n,)), dma((2, 2)), dma((2, 2)), dma((2, 2)), dma((2, 2)),
            dma((2, n)), dma((2, n)), dma((2, ng)), dma((2, ng)),
        ],
        compiler_params=pltpu.CompilerParams(collective_id=1, has_side_effects=True, vmem_limit_bytes=BIG),
        name="barotropic",
    )(table, depths, msg)


def on_device(n, ng, heat, salt, flux, dfac, ids, slot_depth, grid_depth):
    strips, table, depths, coef, nflat, fflat = strips_call(n, ng, flux, dfac, ids, slot_depth, grid_depth)
    heat_new, salt_new, msg = columns_call(n, ng, heat, salt, ids, coef, fflat, nflat, strips)
    height, misfit = barotropic_call(n, ng, table, depths, msg)
    return heat_new, salt_new, height, misfit


def solution(mesh):
    n, ng = mesh.shape["gx"], mesh.shape["gy"]
    slots = P(("gx", "gy"), None)
    cube = P(("gx", "gy"), None, None)
    grid = P("gy", "gx")
    return jax.shard_map(
        functools.partial(on_device, n, ng),
        mesh=mesh,
        in_specs=(cube, cube, slots, P(), P(("gx", "gy")), slots, grid),
        out_specs=(cube, cube, grid, grid),
        check_vma=False,
    )
```

```python
import functools

import jax
import jax.numpy as jnp
from jax import lax
from jax.experimental import pallas as pl
from jax.experimental.pallas import tpu as pltpu
from jax.sharding import PartitionSpec as P

SPAN_E = 60
SPAN_N = 50
KX = 3
KY = 6
LEVELS = 30
SLOTS = KX * KY
CELLS = SPAN_E * SPAN_N
ROWS = KY * SPAN_N
COLS = KX * SPAN_E
TILES = 24
HALINE = 0.8
THERMAL = 0.6
DAMPING = 0.05

BIG = 56 * 2**20
TOP = 16
PLANE = 328
UROWS = TOP + SPAN_N * 8
BLK = 32
EAST = COLS - 128
MESH = pl.DeviceIdType.MESH
F32 = jnp.float32
I32 = jnp.int32
VMEM = pltpu.VMEM


def iota(shape, dim):
    return lax.broadcasted_iota(I32, shape, dim)


def lroll(x, shift):
    shift = shift % x.shape[1]
    return x if shift == 0 else pltpu.roll(x, shift, 1)


def sroll(x, shift):
    shift = shift % x.shape[0]
    return x if shift == 0 else pltpu.roll(x, shift, 0)


def lreverse(x):
    lane = iota(x.shape, 1)
    bit = 1
    while bit < 128:
        x = jnp.where((lane & bit) != 0, lroll(x, bit), lroll(x, -bit))
        bit *= 2
    return x


def flip_cols(a, b):
    ra, rb = lreverse(b), lreverse(a)
    shift = 256 - COLS
    lane = iota(a.shape, 1)
    xa, xb = lroll(ra, -shift), lroll(rb, -shift)
    return jnp.where(lane < 128 - shift, xa, xb), jnp.where(lane < 128 - shift, xb, xa)


def message_rows(cap):
    return cap * TILES + (cap * 3 + 7) // 8 * 8


def greet(peers):
    sem = pltpu.get_barrier_semaphore()
    for peer in peers:
        pl.semaphore_signal(sem, inc=1, device_id=peer, device_id_type=MESH)
    return lambda: pl.semaphore_wait(sem, len(peers))


class Exchange:
    def __init__(self, n, ng, g, y, row_out, row_in, col_out, col_in, row_s, row_r, col_s, col_r):
        self.n, self.ng, self.g, self.y = n, ng, g, y
        self.row_out, self.row_in, self.col_out, self.col_in = row_out, row_in, col_out, col_in
        self.row_s, self.row_r, self.col_s, self.col_r = row_s, row_r, col_s, col_r
        self.lane, self.sub = iota((8, 128), 1), iota((8, 128), 0)
        self.top = lax.div(y + 1, ng)

    def copies(self, k):
        n, ng, g, y, top = self.n, self.ng, self.g, self.y, self.top
        center = g + top * (n - 1 - 2 * g)
        result = []
        for place, d in ((0, 0), (1, 1), (2, -1)):
            target = lax.rem(center + d + n, n)
            up = pltpu.make_async_remote_copy(
                self.row_out.at[k, 0], self.row_in.at[k, top, place], self.row_s.at[k, 0, place],
                self.row_r.at[k, top, place], device_id=(target, y + 1 - top), device_id_type=MESH,
            )
            down, under = [
                pltpu.make_async_remote_copy(
                    self.row_out.at[k, 1], self.row_in.at[k, into, place], self.row_s.at[k, 1, place],
                    self.row_r.at[k, into, place],
                    device_id=(lax.rem(g + d + n, n), lax.rem(y + ng - 1, ng)), device_id_type=MESH,
                )
                for into in (1, 0)
            ]
            mine = None if d == 0 else (y == ng - 1) & (target == g)
            result.append((place, up, down, under, mine))
        cols = [
            pltpu.make_async_remote_copy(
                self.col_out.at[k, slot], self.col_in.at[k, slot], self.col_s.at[k, slot], self.col_r.at[k, slot],
                device_id=(target, y), device_id_type=MESH,
            )
            for slot, target in ((0, lax.rem(g + 1, n)), (1, lax.rem(g + n - 1, n)))
        ]
        return result, cols

    def pack(self, k, plane, caps=None):
        lane, sub = self.lane, self.sub
        north = [plane[half, 312:320, :] for half in range(2)]
        south = [plane[half, 16:24, :] for half in range(2)]
        turned = [
            jnp.where(
                sub < 2,
                jnp.where(sub == 0, sroll(v, -3), sroll(v, -1)),
                jnp.where(sub == 2, sroll(v, 1), sroll(v, 3)),
            )
            for v in north
        ]
        if caps is not None:
            for half in range(2):
                north[half] = jnp.where(sub == 5, caps[0][half], north[half])
                turned[half] = jnp.where(sub == 5, caps[0][half], turned[half])
                south[half] = jnp.where(sub == 5, caps[1][half], south[half])
        flipped = list(flip_cols(*turned))
        flipped[1] = jnp.where(
            lane == 60, lroll(turned[1], -1), jnp.where(lane == 61, lroll(turned[1], 1), flipped[1])
        )
        for half in range(2):
            self.row_out[k, 0, half] = jnp.where(self.y == self.ng - 1, flipped[half], north[half])
            self.row_out[k, 1, half] = south[half]
        for part in range(2):
            to_east = jnp.zeros((8, 128), F32)
            to_west = jnp.zeros((8, 128), F32)
            for t in range(32 * part, min(39, 32 * part + 32)):
                first = 4 * (t - 32 * part)
                here = (lane >= first) & (lane < first + 4)
                rows = slice(8 + 8 * t, 16 + 8 * t)
                a, b = plane[0, rows, :], plane[1, rows, :]
                east, west = lroll(b, first - (EAST - 4)), lroll(a, first)
                if caps is not None:
                    east = jnp.where(lane == first + 3, lroll(b, first + 3 - 60), lroll(b, first - (EAST - 3)))
                    west = jnp.where(lane == first + 3, lroll(b, first + 3 - 61), west)
                to_east = jnp.where(here, east, to_east)
                to_west = jnp.where(here, west, to_west)
            if part == 1 and caps is not None:
                here = (lane >= 64) & (lane < 67)
                both = [jnp.where(sub == 0, caps[0][half], caps[1][half]) for half in range(2)]
                to_east = jnp.where(here, lroll(both[1], 64 - (EAST - 3)), to_east)
                to_west = jnp.where(here, lroll(both[0], 64), to_west)
            self.col_out[k, 0, 8 * part : 8 * part + 8, :] = to_east
            self.col_out[k, 1, 8 * part : 8 * part + 8, :] = to_west

    def start(self, k):
        rows, cols = self.copies(k)
        for copy in cols:
            copy.start()
        for place, up, down, under, mine in rows:
            if mine is None:
                up.start()
            else:

                @pl.when(jnp.logical_not(mine))
                def _(up=up):
                    up.start()

                @pl.when(mine)
                def _(place=place):
                    self.row_in[k, 1, place] = self.row_out[k, 0]

            @pl.when(self.y > 0)
            def _(down=down):
                down.start()

        return rows, cols

    def wait(self, k, started):
        rows, cols = started
        for copy in cols:
            copy.wait()
        for place, up, down, under, mine in rows:
            if mine is None:
                up.wait_send()
                down.wait_recv()
            else:

                @pl.when(jnp.logical_not(mine))
                def _(up=up, down=down):
                    up.wait_send()
                    down.wait_recv()

            @pl.when(self.y > 0)
            def _(down=down, under=under):
                down.wait_send()
                under.wait_recv()

            @pl.when(self.y == 0)
            def _(place=place):
                self.row_in[k, 0, place] = jnp.zeros((2, 8, 128), F32)

    def unpack(self, k, plane, caps=None):
        lane, sub = self.lane, self.sub
        for part in range(2):
            west = self.col_in[k, 0, 8 * part : 8 * part + 8, :]
            east = self.col_in[k, 1, 8 * part : 8 * part + 8, :]
            for t in range(max(1, 32 * part), min(39, 32 * part + 32)):
                first = 4 * (t - 32 * part)
                rows = slice(8 + 8 * t, 16 + 8 * t)
                value = plane[1, rows, :]
                if caps is None:
                    value = jnp.where(lane >= 124, lroll(west, 124 - first), value)
                    value = jnp.where((lane >= EAST) & (lane < EAST + 4), lroll(east, EAST - first), value)
                else:
                    value = jnp.where(lane >= 125, lroll(west, 125 - first), value)
                    value = jnp.where((lane >= EAST) & (lane < EAST + 3), lroll(east, EAST - first), value)
                    value = jnp.where(lane == 62, lroll(east, 62 - first - 3), value)
                    value = jnp.where(lane == 63, lroll(west, 63 - first - 3), value)
                plane[1, rows, :] = value
        found = []
        for side in range(2):
            c, w, e = [[self.row_in[k, side, place, half] for half in range(2)] for place in range(3)]
            tail = jnp.where(lane >= 124, lroll(w[1], 76), c[1])
            tail = jnp.where((lane >= EAST) & (lane < EAST + 4), lroll(e[0], EAST), tail)
            tail = jnp.where(lane == 62, lroll(e[1], 1), jnp.where(lane == 63, lroll(w[1], 3), tail))
            found.append((c[0], tail))
        for half in range(2):
            plane[half, 8:16, :] = sroll(found[0][half], 4)
            plane[half, 312:320, :] = jnp.where(sub < 4, plane[half, 312:320, :], sroll(found[1][half], 4))
        if caps is None:
            return
        west, east = self.col_in[k, 0, 8:16, :], self.col_in[k, 1, 8:16, :]
        line = lane[0:1]
        for half in range(2):
            for which, row in ((0, 316), (1, 15)):
                value = caps[which][half]
                if half == 1:
                    value = jnp.where(line >= 125, lroll(west, 125 - 64)[which : which + 1], value)
                    value = jnp.where(
                        (line >= EAST) & (line < EAST + 3), lroll(east, EAST - 64)[which : which + 1], value
                    )
                plane[half, row : row + 1, :] = plane[half, row : row + 1, :] + value
            for side, row in ((1, 315), (0, 16)):
                value = found[side][half][5:6]
                if half == 1:
                    value = jnp.where((line < EAST + 3) | (line >= 125), value, 0.0)
                plane[half, row : row + 1, :] = plane[half, row : row + 1, :] + value


IDS = 36
MIRROR = 37
SIBLING = 40
OTHER = 48
STRIP_ROWS = 56


def strips_kernel(n, ng, cap, ids_ref, dfac_ref, depth_hbm, slot_hbm, flux_hbm,
                  all_ref, tab_ref, dpl, coef, nflat, fflat,
                  depth_ref, slot_ref, flux_ref, wide, msg, edge, got,
                  row_out, row_in, col_out, col_in,
                  own, s1, r1, s2, r2, s3, r3, row_s, row_r, col_s, col_r):
    g = lax.axis_index("gx")
    y = lax.axis_index("gy")
    loads = [
        pltpu.make_async_copy(src, dst, own.at[k])
        for k, (src, dst) in enumerate(((depth_hbm, depth_ref), (slot_hbm, slot_ref), (flux_hbm, flux_ref)))
    ]
    for load in loads:
        load.start()
    odd = lax.rem(y, 2)
    sibling = y + 1 - 2 * odd
    other = lax.rem(y + ng + 2 * odd - 1, ng)
    band = [(lax.rem(g + k, n), y) for k in range(1, n)]
    beside = [(lax.rem(g + k, n), other) for k in range(n)]
    corners = [(lax.rem(g + k, n), sibling) for k in (0, 1, n - 1)]
    everyone = greet(band + beside + corners)
    exchange = Exchange(n, ng, g, y, row_out, row_in, col_out, col_in, row_s, row_r, col_s, col_r)
    lane = iota((8, 128), 1)
    row = iota((1, 128), 1)
    code = jnp.full((1, 128), -1, I32)
    owners = []
    for s in range(SLOTS):
        block = jnp.maximum(ids_ref[s], 0)
        bx = lax.rem(block, KX * n)
        by = lax.rem(lax.div(block, KX * n), KY)
        owner = jnp.where(ids_ref[s] >= 0, lax.div(bx, KX), -1)
        rank = jnp.int32(0)
        for other in owners:
            rank = rank + jnp.where(other == owner, 1, 0)
        owners.append(owner)
        value = (owner * 32 + by * KX + lax.rem(bx, KX)) * 32 + rank
        code = jnp.where(row == s, jnp.where(owner >= 0, value, -1), code)
    loads[0].wait()
    for half in range(2):
        dpl[half, 0:16, :] = jnp.zeros((16, 128), F32)
        dpl[half, 312:UROWS, :] = jnp.zeros((UROWS - 312, 128), F32)
    wide[...] = jnp.zeros(wide.shape, F32)
    wide[0:COLS, 0:ROWS] = depth_ref[...].astype(F32)
    for half in range(2):
        for third in range(3):
            turned = wide[128 * half : 128 * half + 128, 128 * third : 128 * third + 128].T
            rows = min(128, ROWS - 128 * third)
            dpl[half, TOP + 128 * third : TOP + 128 * third + rows, :] = turned[0:rows]
    rims = [jnp.zeros((8, 128), F32) for _ in range(KX)]
    ns = []
    for i in range(SPAN_N):
        off = SPAN_E * i % 128
        a = dpl[0, pl.ds(TOP + i, 8, stride=SPAN_N), :]
        b = dpl[1, pl.ds(TOP + i, 8, stride=SPAN_N), :]
        cells = [a, a, jnp.where(lane < 64, b, a)]
        push = 0 if i < 32 else 1
        first, last = (off + push) % 128, (off + SPAN_E - 1 - push) % 128
        for bx in range(KX):
            turn = off - SPAN_E * bx
            rims[bx] = jnp.where(lane == first, lroll(cells[bx], turn + push), rims[bx])
            rims[bx] = jnp.where(lane == last, lroll(cells[bx], turn - push), rims[bx])
        if i == 0:
            ns = [lroll(cells[bx], -SPAN_E * bx) for bx in range(KX)]
        if i == SPAN_N - 1:
            ns = [
                jnp.where(lane < SPAN_E, ns[bx], lroll(cells[bx], SPAN_E - SPAN_E * bx))
                for bx in range(KX)
            ]
    ns = [v.astype(I32) for v in ns]
    for bx in range(KX):
        for part, value in enumerate((rims[bx].astype(I32), ns[bx])):
            msg[pl.ds(bx * 2 + part, 8, stride=6), :] = value
    msg[IDS : IDS + 1, :] = code
    edge[...] = jnp.zeros((8, 128), I32)
    for bx in range(KX):
        msg[MIRROR + bx : MIRROR + bx + 1, :] = lroll(lreverse(ns[bx]), -8)[KY - 1 : KY]
        edge[bx : bx + 1, :] = ns[bx][0:1]
        edge[3 + bx : 4 + bx, :] = ns[bx][KY - 1 : KY]
    exchange.pack(0, dpl)

    everyone()
    near = pltpu.make_async_remote_copy(
        edge, got, s1.at[0], r1.at[0], device_id=(g, sibling), device_id_type=MESH
    )
    near.start()
    sends = []
    for k, peer in enumerate(beside):
        copy = pltpu.make_async_remote_copy(
            edge, all_ref.at[g, pl.ds(OTHER, 8)], s3.at[k], r3.at[k], device_id=peer, device_id_type=MESH
        )
        copy.start()
        sends.append(copy)
    near.wait()
    msg[SIBLING : SIBLING + 8, :] = got[...]
    for k, peer in enumerate(band):
        copy = pltpu.make_async_remote_copy(
            msg, all_ref.at[g, pl.ds(0, OTHER)], s2.at[k], r2.at[k], device_id=peer, device_id_type=MESH
        )
        copy.start()
        sends.append(copy)
    halo = exchange.start(0)
    all_ref[pl.ds(g, 1), 0:OTHER] = msg[...][None]
    gain = jnp.zeros((1, 128), F32)
    for k in range(LEVELS):
        above = dfac_ref[k - 1] if k > 0 else jnp.float32(0)
        below = dfac_ref[k] if k + 1 < LEVELS else jnp.float32(0)
        base = (1.0 + above) - above * gain
        full = 1.0 / (base + below)
        gain = below * full
        coef[0, k : k + 1, :] = full
        coef[1, k : k + 1, :] = 1.0 / base
        coef[2, k : k + 1, :] = jnp.broadcast_to(above, (1, 128))
        coef[3, k : k + 1, :] = gain
    loads[1].wait()
    loads[2].wait()
    for t in range(TILES):
        width = min(128, CELLS - 128 * t)
        span = slice(t * 128, t * 128 + width)
        for first in (0, 8, 16):
            number = min(8, SLOTS - first)
            place = pl.ds(first * TILES + t, number, stride=TILES)
            for src, dst, kind in ((slot_ref, nflat, I32), (flux_ref, fflat, F32)):
                value = src[first : first + number, span]
                if width < 128:
                    value = jnp.concatenate([value, jnp.zeros((number, 128 - width), kind)], axis=1)
                dst[place, :] = value
    exchange.wait(0, halo)
    exchange.unpack(0, dpl)
    for copy in sends:
        copy.wait()
    codes = all_ref[:, IDS, :]
    key = codes >> 5
    rank = codes & 31
    source = iota((n, 128), 0)
    number = (source * cap + rank + 1).astype(F32)
    for p in range(SLOTS):
        hit = jnp.where(key == g * 32 + p, number, 0.0)
        hit = jnp.sum(jnp.sum(hit, axis=0, keepdims=True), axis=1, keepdims=True)
        tab_ref[p : p + 1, :] = jnp.broadcast_to(hit.astype(I32) - 1, (1, 128))
    tab_ref[SLOTS:24, :] = jnp.full((24 - SLOTS, 128), -1, I32)


def ahead(x, step):
    a = lroll(x, -step)
    return jnp.where(iota(x.shape, 1) < 128 - step, a, sroll(a, -1))


def behind(x, step):
    a = lroll(x, step)
    return jnp.where(iota(x.shape, 1) >= step, a, sroll(a, 1))


STEP = 33
AHEAD = 5


def columns_kernel(n, ng, cap, ids_ref, coef, fflat, nflat, strips_ref, heat_hbm, salt_hbm,
                   heat_out, salt_out, msg_ref, heat_in, salt_in, jcol, inh, ins, yh, ys, oh, os_, count, sems):
    step = pl.program_id(0)
    shape = (TILES, 128)
    row24 = iota(shape, 0)
    lane24 = iota(shape, 1)
    cell = row24 * 128 + lane24
    lane = iota((1, 128), 1)
    last = CELLS - 128 * (TILES - 1)

    ring = AHEAD + 1

    def loads(slot):
        place = lax.rem(slot, ring)
        return [
            pltpu.make_async_copy(src.at[slot], dst.at[place], sems.at[place, which])
            for which, (src, dst) in enumerate(((heat_hbm, heat_in), (salt_hbm, salt_in)))
        ]

    @pl.when(step == 0)
    def _():
        for slot in range(AHEAD):
            for load in loads(slot):
                load.start()
        flat = cell.astype(F32)
        whole = jnp.floor((flat + 0.5) * (1.0 / SPAN_E))
        jcol[...] = cell - whole.astype(I32) * SPAN_E
        for d in range(n):
            count[d] = 0

    @pl.when(step + AHEAD < SLOTS)
    def _():
        for load in loads(step + AHEAD):
            load.start()

    for load in loads(step):
        load.wait()
    here = lax.rem(step, ring)
    for t in range(TILES):
        width = 128 if t < TILES - 1 else last
        cols = slice(t * 128, t * 128 + width)
        inh[t * STEP : t * STEP + LEVELS, 0:width] = heat_in[here, :, cols]
        ins[t * STEP : t * STEP + LEVELS, 0:width] = salt_in[here, :, cols]

    mine = pl.ds(pl.multiple_of(step * TILES, 8), TILES)
    depth = nflat[mine, :]
    wet = depth > 0
    h = s = None
    for k in range(LEVELS):
        level = pl.ds(k, TILES, stride=STEP)
        rh = inh[level, :]
        rs = ins[level, :]
        deeper = depth > k + 1
        if k == 0:
            rh = rh + jnp.where(wet, fflat[mine, :], 0.0)
            pivot = jnp.where(deeper, coef[0, 0:1, :], 1.0)
            h = rh * pivot
            s = rs * pivot
        else:
            above = jnp.where(wet, coef[2, k : k + 1, :], 0.0)
            pivot = jnp.where(wet, coef[1, k : k + 1, :], 1.0)
            if k + 1 < LEVELS:
                pivot = jnp.where(deeper, coef[0, k : k + 1, :], pivot)
            h = (rh + above * h) * pivot
            s = (rs + above * s) * pivot
        if k + 1 < LEVELS:
            yh[k * TILES : (k + 1) * TILES, :] = h
            ys[k * TILES : (k + 1) * TILES, :] = s
        wet = deeper
    level = pl.ds(LEVELS - 1, TILES, stride=STEP)
    oh[level, :] = h
    os_[level, :] = s
    for k in range(LEVELS - 2, -1, -1):
        gain = jnp.where(depth > k + 1, coef[3, k : k + 1, :], 0.0)
        h = yh[k * TILES : (k + 1) * TILES, :] + gain * h
        s = ys[k * TILES : (k + 1) * TILES, :] + gain * s
        level = pl.ds(k, TILES, stride=STEP)
        oh[level, :] = h
        os_[level, :] = s
    for t in range(TILES):
        width = 128 if t < TILES - 1 else last
        cols = slice(t * 128, t * 128 + width)
        heat_out[0, :, cols] = oh[t * STEP : t * STEP + LEVELS, 0:width]
        salt_out[0, :, cols] = os_[t * STEP : t * STEP + LEVELS, 0:width]

    blocks_x = KX * n
    ident = ids_ref[step]
    block = jnp.maximum(ident, 0)
    bx = lax.rem(block, blocks_x)
    by = lax.div(block, blocks_x)
    byl = lax.rem(by, KY)
    dev = lax.div(bx, KX)
    bxl = lax.rem(bx, KX)

    def strip(device, place):
        return strips_ref[device, pl.ds(place, 1), :]

    def rim_of(col):
        return strip(lax.div(col, KX), (byl * KX + lax.rem(col, KX)) * 2)

    east = rim_of(lax.rem(bx + 1, blocks_x))
    west = rim_of(lax.rem(bx + blocks_x - 1, blocks_x))
    ew = [
        jnp.where((lane & 3) == 3, lroll(east, SPAN_E - 1 - push), lroll(west, 1 - SPAN_E + push))
        for push in range(2)
    ]
    ew = jnp.where(row24 < 15, ew[0], ew[1])
    mirror = blocks_x - 1 - bx
    mirrored = lax.rem(mirror, KX)
    folded = by == KY * ng - 1
    inner = byl < KY - 1
    even = lax.rem(lax.div(by, KY), 2) == 0
    north_dev = jnp.where(folded, lax.div(mirror, KX), dev)
    north_row = jnp.where(
        inner,
        ((byl + 1) * KX + bxl) * 2 + 1,
        jnp.where(folded, MIRROR + mirrored, jnp.where(even, SIBLING, OTHER) + bxl),
    )
    north = lroll(strip(north_dev, north_row), -4)
    south_row = jnp.where(byl > 0, ((byl - 1) * KX + bxl) * 2 + 1, jnp.where(even, OTHER, SIBLING) + 3 + bxl)
    south = jnp.where(by > 0, lroll(strip(dev, south_row), -SPAN_E), 0)
    j = jcol[...]
    inside = cell < CELLS
    first_j = j == 0
    last_j = j == SPAN_E - 1
    first_i = cell < SPAN_E
    last_i = cell >= CELLS - SPAN_E
    faces = (
        jnp.minimum(depth, jnp.where(last_j, ew, ahead(depth, 1))),
        jnp.minimum(depth, jnp.where(first_j, ew, behind(depth, 1))),
        jnp.minimum(depth, jnp.where(last_i, north, ahead(depth, SPAN_E))),
        jnp.minimum(depth, jnp.where(first_i, south, behind(depth, SPAN_E))),
    )
    sums = [jnp.zeros(shape, F32) for _ in range(4)]
    pressure = jnp.zeros(shape, F32)
    total = jnp.zeros(shape, F32)
    for k in range(LEVELS):
        level = pl.ds(k, TILES, stride=STEP)
        pressure = pressure + (HALINE * os_[level, :] - THERMAL * oh[level, :])
        total = total + pressure
        sums = [jnp.where(face == k + 1, total, held) for face, held in zip(faces, sums)]
    sums = [jnp.where(inside, held, 0.0) for held in sums]
    se, sw, sn, ss = sums
    local = jnp.where(last_j, 0.0, ahead(sw, 1)) - se
    local = local + (jnp.where(first_j, 0.0, behind(se, 1)) - sw)
    local = local + (jnp.where(last_i, 0.0, ahead(ss, SPAN_E)) - sn)
    local = local + (jnp.where(first_i, 0.0, behind(sn, SPAN_E)) - ss)
    local = jnp.where(inside, local, 0.0)
    rim = jnp.where(last_j, se, jnp.where(first_j, sw, 0.0))
    rim0 = jnp.sum(jnp.where(row24 < 15, rim, 0.0), axis=0, keepdims=True)
    rim1 = jnp.sum(jnp.where(row24 >= 15, rim, 0.0), axis=0, keepdims=True)
    top = jnp.sum(jnp.where(last_i, sn, 0.0), axis=0, keepdims=True)
    bottom = jnp.sum(jnp.where(first_i, ss, 0.0), axis=0, keepdims=True)
    cap_row = jnp.where(lane < SPAN_E, bottom, jnp.where(lane < 2 * SPAN_E, lroll(top, 64), 0.0))

    @pl.when(ident >= 0)
    def _():
        rank = count[dev]
        count[dev] = rank + 1
        msg_ref[dev, pl.ds(pl.multiple_of(rank * TILES, 8), TILES), :] = local
        base = cap * TILES + rank * 3
        for part, value in enumerate((rim0, rim1, cap_row)):
            msg_ref[dev, pl.ds(base + part, 1), :] = value


def barotropic_kernel(n, ng, cap, tab_ref, dpl, msg_ref, height_ref, misfit_ref,
                      recv, blk, upl, zpl, wts, qpl, row_out, row_in, col_out, col_in,
                      red_out, red_x, red_y, own_sem, a2a_s, a2a_r, row_s, row_r, col_s, col_r,
                      rx_s, rx_r, ry_s, ry_r):
    g = lax.axis_index("gx")
    y = lax.axis_index("gy")
    band = [(lax.rem(g + k, n), y) for k in range(1, n)]
    column = [(g, lax.rem(y + k, ng)) for k in range(1, ng)]
    corners = [(lax.rem(g + a, n), lax.rem(y + b, ng)) for a in (1, n - 1) for b in (1, ng - 1)]
    everyone = greet(band + column + corners)
    exchange = Exchange(n, ng, g, y, row_out, row_in, col_out, col_in, row_s, row_r, col_s, col_r)
    lane = iota((8, 128), 1)
    sub = iota((8, 128), 0)
    zero8 = jnp.zeros((8, 128), F32)
    for half in range(2):
        for ref in (zpl, qpl.at[0], qpl.at[1], qpl.at[2], qpl.at[3]):
            ref[half, 0:8, :] = zero8
            ref[half, 320:PLANE, :] = zero8

    span = 24
    chunks = 13
    lane_c = iota((span, 128), 1)

    def rows_at(t, shift=0):
        return pl.ds(8 + t * span + shift, span)

    def both(ref, rows):
        return [ref[half, rows, :] for half in range(2)]

    def from_east(pair):
        a, b = [lroll(v, -1) for v in pair]
        return jnp.where(lane_c < 127, a, b), jnp.where(lane_c < 127, b, a)

    def from_west(pair):
        a, b = [lroll(v, 1) for v in pair]
        return jnp.where(lane_c >= 1, a, b), jnp.where(lane_c >= 1, b, a)

    def weigh(t, carry):
        rows = rows_at(t)
        d = both(dpl, rows)
        beside = (from_east(d), from_west(d), both(dpl, rows_at(t, 1)), both(dpl, rows_at(t, -1)))
        r = iota((span, 128), 0) + (8 + t * span)
        for half in range(2):
            damp = jnp.where(d[half] > 0, DAMPING, 1.0)
            diagonal = damp
            for side in range(4):
                w = jnp.minimum(d[half], beside[side][half]) * (1.0 / LEVELS)
                wts[side, half, rows, :] = w
                diagonal = diagonal + w
            inverse = 1.0 / diagonal
            wts[4, half, rows, :] = damp
            wts[5, half, rows, :] = inverse
            inside = (r >= TOP) & (r < TOP + ROWS)
            if half == 1:
                inside = inside & (lane_c < EAST)
            wts[6, half, rows, :] = jnp.where(inside, inverse, 0.0)
        return carry

    lax.fori_loop(0, chunks, weigh, 0)

    everyone()
    own = pltpu.make_async_copy(msg_ref.at[g], recv.at[g], own_sem)
    own.start()
    sends = []
    for k, peer in enumerate(band):
        copy = pltpu.make_async_remote_copy(
            msg_ref.at[peer[0]], recv.at[g], a2a_s.at[k], a2a_r.at[k], device_id=peer, device_id_type=MESH
        )
        copy.start()
        sends.append(copy)


    own.wait()
    for copy in sends:
        copy.wait()
    for bx in range(KX):
        blk[(bx * 8 + KY) * BLK : (bx + 1) * 8 * BLK, :] = jnp.zeros((2 * BLK, 128), F32)
        wanted = [
            jnp.broadcast_to(tab_ref[by * KX + bx : by * KX + bx + 1, :], (8, 128)) for by in range(KY)
        ]

        def pick(source, held, wanted=wanted):
            held = list(held)
            for rank in range(cap):
                parts = [recv[source, rank * TILES + 8 * v : rank * TILES + 8 * v + 8, :] for v in range(3)]
                first = cap * TILES + rank * 3
                rest = recv[source, first : first + 3, :]
                for by in range(KY):
                    hit = wanted[by] == source * cap + rank
                    for v in range(3):
                        held[by * 4 + v] = jnp.where(hit, parts[v], held[by * 4 + v])
                    held[by * 4 + 3] = jnp.where(hit[0:3], rest, held[by * 4 + 3])
            return tuple(held)

        start = ([zero8] * 3 + [jnp.zeros((3, 128), F32)]) * KY
        held = lax.fori_loop(0, n, pick, tuple(start))
        for by in range(KY):
            base = (bx * 8 + by) * BLK
            for v in range(3):
                blk[base + 8 * v : base + 8 * v + 8, :] = held[by * 4 + v]
            blk[base + TILES : base + TILES + 3, :] = held[by * 4 + 3]

    def rows_of(bx, row):
        return blk[pl.ds(bx * 8 * BLK + row, 8, stride=BLK), :]

    rims = [[rows_of(bx, TILES + part) for part in range(2)] for bx in range(KX)]
    cap_rows = [rows_of(bx, TILES + 2) for bx in range(KX)]

    def lay(v):
        tail = jnp.where(lane < EAST, v[2], 0.0)
        return jnp.where(lane < 60, v[0], jnp.where(lane < 120, v[1], v[2])), tail

    souths = lay([lroll(cap_rows[bx], SPAN_E * bx) for bx in range(KX)])
    norths = lay([lroll(cap_rows[bx], SPAN_E * bx - SPAN_E) for bx in range(KX)])
    for i in range(SPAN_N):
        t, off = SPAN_E * i // 128, SPAN_E * i % 128
        cells = []
        for bx in range(KX):
            value = rows_of(bx, t)
            if off + SPAN_E > 128:
                value = jnp.where(lane >= off, value, rows_of(bx, t + 1))
            cells.append(lroll(value, SPAN_E * bx - off))
        first, second = lay(cells)
        second = jnp.where(
            lane == 60,
            lroll(rims[KX - 1][i // 32], 61 - SPAN_E - off),
            jnp.where(lane == 61, lroll(rims[0][i // 32], 61 - off), second),
        )
        rim = [rims[bx][i // 32] for bx in range(KX)]
        first = first + jnp.where(
            lane == 59,
            lroll(rim[1], 59 - off),
            jnp.where(
                lane == 60,
                lroll(rim[0], 1 - off),
                jnp.where(lane == 119, lroll(rim[2], 119 - off), jnp.where(lane == 120, lroll(rim[1], 61 - off), 0.0)),
            ),
        )
        if i == SPAN_N - 1:
            first = first + jnp.where(sub < KY - 1, sroll(souths[0], -1), 0.0)
            second = second + jnp.where(sub < KY - 1, sroll(souths[1], -1), 0.0)
        if i == 0:
            first = first + jnp.where((sub > 0) & (sub < KY), sroll(norths[0], 1), 0.0)
            second = second + jnp.where((sub > 0) & (sub < KY), sroll(norths[1], 1), 0.0)
        upl[0, pl.ds(TOP + i, 8, stride=SPAN_N), :] = first
        upl[1, pl.ds(TOP + i, 8, stride=SPAN_N), :] = second
    for half in range(2):
        upl[half, 8:16, :] = zero8
    caps = ([v[KY - 1 : KY] for v in norths], [v[0:1] for v in souths])
    exchange.pack(0, upl, caps)
    exchange.wait(0, exchange.start(0))
    exchange.unpack(0, upl, caps)

    def begin(t, carry):
        rows = rows_at(t)
        a, b = both(upl, rows)
        a = a + jnp.where(lane_c == 0, lroll(b, -63), 0.0)
        b = b + jnp.where(
            lane_c == EAST - 1,
            lroll(b, EAST - 1 - 62),
            jnp.where(lane_c == EAST, lroll(b, EAST - 60), jnp.where(lane_c == 127, lroll(b, 127 - 61), 0.0)),
        )
        for half, value in enumerate((a, b)):
            rhs = value * (1.0 / LEVELS)
            qpl[0, half, rows, :] = rhs
            zpl[half, rows, :] = rhs * wts[5, half, rows, :]
        return carry

    lax.fori_loop(0, chunks, begin, 0)

    def image(out, scale_next):
        def body(t, carry):
            rows = rows_at(t)
            v = both(zpl, rows)
            beside = (from_east(v), from_west(v), both(zpl, rows_at(t, 1)), both(zpl, rows_at(t, -1)))
            for half in range(2):
                result = wts[4, half, rows, :] * v[half]
                for side in range(4):
                    result = result + wts[side, half, rows, :] * (v[half] - beside[side][half])
                qpl[out, half, rows, :] = result
            return carry

        lax.fori_loop(0, chunks, body, 0)
        if scale_next:

            def scale(t, carry):
                rows = rows_at(t)
                for half in range(2):
                    zpl[half, rows, :] = qpl[out, half, rows, :] * wts[5, half, rows, :]
                return carry

            lax.fori_loop(0, chunks, scale, 0)

    image(1, True)
    image(2, True)
    image(3, False)

    def fold3(v):
        return v[0:8] + v[8:16] + v[16:24]

    def first_dots(t, carry):
        rows = rows_at(t)
        a, b = carry
        for half in range(2):
            z = qpl[0, half, rows, :] * wts[6, half, rows, :]
            a = a + fold3(qpl[0, half, rows, :] * z)
            b = b + fold3(qpl[1, half, rows, :] * z)
        return a, b

    def splat(v):
        v = jnp.sum(jnp.sum(v, axis=0, keepdims=True), axis=1, keepdims=True)
        return jnp.broadcast_to(v, (8, 128))

    mass, curve = [splat(v) for v in lax.fori_loop(0, chunks, first_dots, (zero8, zero8))]
    own_ray = jnp.where(mass > 0, jnp.clip(curve / jnp.where(mass > 0, mass, 1.0), 0.0, 2.0), 0.0)
    ray_c = jnp.broadcast_to(own_ray[0:1], (span, 128))
    pairs = ((0, 0), (1, 0), (2, 0), (3, 0), (1, 1), (2, 1), (3, 1), (2, 2), (3, 2))

    def shift(t, carry):
        rows = rows_at(t)
        c = list(carry)
        for half in range(2):
            w0, w1, w2, w3 = [qpl[j, half, rows, :] for j in range(4)]
            q1 = w1 - ray_c * w0
            t2 = w2 - ray_c * w1
            t3 = (w3 - ray_c * w2) - ray_c * t2
            q2 = t2 - ray_c * q1
            q3 = t3 - ray_c * q2
            qpl[1, half, rows, :] = q1
            qpl[2, half, rows, :] = q2
            qpl[3, half, rows, :] = q3
            q = (w0, q1, q2, q3)
            inverse = wts[6, half, rows, :]
            z = [v * inverse for v in q[0:3]]
            for place, (i, j) in enumerate(pairs):
                c[place] = c[place] + fold3(q[i] * z[j])
        return tuple(c)

    sums = lax.fori_loop(0, chunks, shift, (zero8,) * len(pairs))
    red_out[0, 0:1, :] = own_ray[0:1]
    red_out[0, 1:2, :] = mass[0:1]
    for place, part in enumerate(sums):
        red_out[0, 2 + place : 3 + place, :] = jnp.sum(part, axis=0, keepdims=True)
    red_out[0, 11:16, :] = jnp.zeros((5, 128), F32)
    for level, (peers, into, sem_s, sem_r, me) in enumerate(
        ((band, red_x, rx_s, rx_r, g), (column, red_y, ry_s, ry_r, y))
    ):
        place = pl.ds(pl.multiple_of(me * 16, 8), 16)
        copies = []
        for number, peer in enumerate(peers):
            copy = pltpu.make_async_remote_copy(
                red_out.at[level], into.at[place], sem_s.at[number], sem_r.at[number],
                device_id=peer, device_id_type=MESH,
            )
            copy.start()
            copies.append(copy)
        into[place, :] = red_out[level]
        for copy in copies:
            copy.wait()
        count = len(peers) + 1
        ray, mass, *old = [into[pl.ds(m, count, stride=16), :] for m in range(2 + len(pairs))]
        total = jnp.sum(mass, axis=0, keepdims=True)
        common = jnp.sum(ray * mass, axis=0, keepdims=True) / total
        common = jnp.where(total > 0, common, 0.0)
        d = ray - common
        terms = [[None] * 4 for _ in range(4)]
        for i, c in enumerate(((1,), (1, 1), (1, 2, 1), (1, 3, 3, 1))):
            for j in range(i + 1):
                power = jnp.full(d.shape, float(c[j]), F32)
                for _ in range(i - j):
                    power = power * d
                terms[i][j] = power
        gram = dict(zip(pairs, old))

        def entry(i, j):
            return gram[(i, j)] if i >= j else gram[(j, i)]

        new = []
        for i, j in pairs:
            value = None
            for a in range(i + 1):
                for b in range(j + 1):
                    term = entry(a, b)
                    if a < i:
                        term = term * terms[i][a]
                    if b < j:
                        term = term * terms[j][b]
                    value = term if value is None else value + term
            new.append(jnp.sum(value, axis=0, keepdims=True))
        if level == 0:
            red_out[1, 0:1, :] = common
            red_out[1, 1:2, :] = total
            for number, part in enumerate(new):
                red_out[1, 2 + number : 3 + number, :] = part
            red_out[1, 11:16, :] = jnp.zeros((5, 128), F32)
    ray = jnp.broadcast_to(common, (8, 128))
    moment = {
        pair: jnp.broadcast_to(jnp.sum(part, axis=1, keepdims=True), (8, 128)) for pair, part in zip(pairs, new)
    }
    norm = moment[(0, 0)]
    moment = [moment[pair] for pair in ((1, 0), (1, 1), (2, 1), (2, 2), (3, 2))]
    one = jnp.ones((8, 128), F32)
    scale = one / norm
    c = [one] + [m * scale for m in moment]
    zero = zero8
    rho = [one, zero, zero, zero]
    pi = [one, zero, zero]
    xs = [zero, zero, zero]
    gamma = one
    for it in range(3):
        curve = zero
        for i in range(it + 1):
            for j in range(it + 1):
                curve = curve + (pi[i] * pi[j]) * (ray * c[i + j] + c[i + j + 1])
        alpha = gamma / curve
        xs = [xs[i] + alpha * pi[i] if i <= it else xs[i] for i in range(3)]
        for i in range(it + 2):
            step = ray * pi[i] if i <= it else zero
            if i > 0:
                step = step + pi[i - 1]
            rho[i] = rho[i] - alpha * step
        if it == 2:
            break
        gamma_new = zero
        for i in range(it + 2):
            for j in range(it + 2):
                gamma_new = gamma_new + (rho[i] * rho[j]) * c[i + j]
        beta = gamma_new / gamma
        pi = [rho[i] + beta * pi[i] for i in range(3)]
        gamma = gamma_new

    d = own_ray - ray
    d2 = d * d
    rho = [
        rho[0] + d * rho[1] + d2 * rho[2] + d2 * d * rho[3],
        rho[1] + 2.0 * d * rho[2] + 3.0 * d2 * rho[3],
        rho[2] + 3.0 * d * rho[3],
        rho[3],
    ]
    xs = [xs[0] + d * xs[1] + d2 * xs[2], xs[1] + 2.0 * d * xs[2], xs[2]]

    def finish(first, size):
        rows = pl.ds(TOP + first, size)
        out = pl.ds(first, size)
        x = [jnp.broadcast_to(v[0:1], (size, 128)) for v in xs]
        r = [jnp.broadcast_to(v[0:1], (size, 128)) for v in rho]
        for half in range(2):
            q = [qpl[j, half, rows, :] for j in range(4)]
            high = (x[0] * q[0] + x[1] * q[1] + x[2] * q[2]) * wts[5, half, rows, :]
            rest = r[0] * q[0] + r[1] * q[1] + r[2] * q[2] + r[3] * q[3]
            if half == 0:
                height_ref[out, 0:128] = high
                misfit_ref[out, 0:128] = rest
            else:
                height_ref[out, 128:COLS] = high[:, 0:EAST]
                misfit_ref[out, 128:COLS] = rest[:, 0:EAST]

    def finish_chunk(t, carry):
        finish(pl.multiple_of(t * span, 8), span)
        return carry

    lax.fori_loop(0, ROWS // span, finish_chunk, 0)
    finish(ROWS // span * span, ROWS % span)


def strips_call(n, ng, flux, dfac, ids, slot_depth, grid_depth):
    vmem = pl.BlockSpec(memory_space=VMEM)
    smem = pl.BlockSpec(memory_space=pltpu.SMEM)
    hbm = pl.BlockSpec(memory_space=pl.ANY)
    dma = pltpu.SemaphoreType.DMA
    flat = (SLOTS * TILES, 128)
    return pl.pallas_call(
        functools.partial(strips_kernel, n, ng, (SLOTS + n - 1) // n),
        out_shape=(
            jax.ShapeDtypeStruct((n, STRIP_ROWS, 128), I32), jax.ShapeDtypeStruct((24, 128), I32),
            jax.ShapeDtypeStruct((2, UROWS, 128), F32), jax.ShapeDtypeStruct((4, 32, 128), F32),
            jax.ShapeDtypeStruct(flat, I32), jax.ShapeDtypeStruct(flat, F32),
        ),
        in_specs=[smem, smem, hbm, hbm, hbm],
        out_specs=(vmem,) * 6,
        scratch_shapes=[
            VMEM((COLS, ROWS), I32), VMEM((SLOTS, CELLS), I32), VMEM((SLOTS, CELLS), F32),
            VMEM((256, 384), F32), VMEM((48, 128), I32), VMEM((8, 128), I32), VMEM((8, 128), I32),
            VMEM((1, 2, 2, 8, 128), F32), VMEM((1, 2, 3, 2, 8, 128), F32),
            VMEM((1, 2, 16, 128), F32), VMEM((1, 2, 16, 128), F32),
            dma((3,)), dma((1,)), dma((1,)), dma((n,)), dma((n,)), dma((n,)), dma((n,)),
            dma((1, 2, 3)), dma((1, 2, 3)), dma((1, 2)), dma((1, 2)),
        ],
        compiler_params=pltpu.CompilerParams(collective_id=0, has_side_effects=True, vmem_limit_bytes=BIG),
        name="strips",
    )(ids, dfac, grid_depth.T, slot_depth, flux)


def columns_call(n, ng, heat, salt, ids, coef, fflat, nflat, strips):
    cap = (SLOTS + n - 1) // n
    msg_rows = message_rows(cap)
    smem = pl.BlockSpec(memory_space=pltpu.SMEM)
    hbm = pl.BlockSpec(memory_space=pl.ANY)
    fixed = lambda shape: pl.BlockSpec(shape, lambda s: (0,) * len(shape))
    block = pl.BlockSpec((1, LEVELS, CELLS), lambda s: (s, 0, 0))
    ring = (AHEAD + 1, LEVELS, CELLS)
    tall = TILES * STEP + 8
    return pl.pallas_call(
        functools.partial(columns_kernel, n, ng, cap),
        grid=(SLOTS,),
        out_shape=(
            jax.ShapeDtypeStruct(heat.shape, F32),
            jax.ShapeDtypeStruct(salt.shape, F32),
            jax.ShapeDtypeStruct((n, msg_rows, 128), F32),
        ),
        in_specs=[
            smem, fixed((4, 32, 128)), fixed((SLOTS * TILES, 128)), fixed((SLOTS * TILES, 128)),
            fixed((n, STRIP_ROWS, 128)), hbm, hbm,
        ],
        out_specs=(block, block, fixed((n, msg_rows, 128))),
        scratch_shapes=[
            VMEM(ring, F32), VMEM(ring, F32), VMEM((TILES, 128), I32),
            VMEM((tall, 128), F32), VMEM((tall, 128), F32),
            VMEM((TILES * LEVELS, 128), F32), VMEM((TILES * LEVELS, 128), F32),
            VMEM((tall, 128), F32), VMEM((tall, 128), F32),
            pltpu.SMEM((n,), I32), pltpu.SemaphoreType.DMA((AHEAD + 1, 2)),
        ],
        compiler_params=pltpu.CompilerParams(vmem_limit_bytes=BIG),
        name="columns",
    )(ids, coef, fflat, nflat, strips, heat, salt)


def barotropic_call(n, ng, table, depths, msg):
    cap = (SLOTS + n - 1) // n
    vmem = pl.BlockSpec(memory_space=VMEM)
    dma = pltpu.SemaphoreType.DMA
    field = jax.ShapeDtypeStruct((ROWS, COLS), F32)
    plane = (2, PLANE, 128)
    return pl.pallas_call(
        functools.partial(barotropic_kernel, n, ng, cap),
        out_shape=(field, field),
        in_specs=[vmem, vmem, pl.BlockSpec(memory_space=pl.ANY)],
        out_specs=(vmem, vmem),
        scratch_shapes=[
            VMEM((n, message_rows(cap), 128), F32), VMEM((KX * 8 * BLK, 128), F32),
            VMEM((2, UROWS, 128), F32), VMEM(plane, F32),
            VMEM((7,) + plane, F32), VMEM((4,) + plane, F32),
            VMEM((1, 2, 2, 8, 128), F32), VMEM((1, 2, 3, 2, 8, 128), F32),
            VMEM((1, 2, 16, 128), F32), VMEM((1, 2, 16, 128), F32),
            VMEM((2, 16, 128), F32), VMEM((n * 16, 128), F32), VMEM((ng * 16, 128), F32),
            dma, dma((n,)), dma((n,)), dma((1, 2, 3)), dma((1, 2, 3)), dma((1, 2)), dma((1, 2)),
            dma((n,)), dma((n,)), dma((ng,)), dma((ng,)),
        ],
        compiler_params=pltpu.CompilerParams(collective_id=1, has_side_effects=True, vmem_limit_bytes=BIG),
        name="barotropic",
    )(table, depths, msg)


def on_device(n, ng, heat, salt, flux, dfac, ids, slot_depth, grid_depth):
    strips, table, depths, coef, nflat, fflat = strips_call(n, ng, flux, dfac, ids, slot_depth, grid_depth)
    heat_new, salt_new, msg = columns_call(n, ng, heat, salt, ids, coef, fflat, nflat, strips)
    height, misfit = barotropic_call(n, ng, table, depths, msg)
    return heat_new, salt_new, height, misfit


def solution(mesh):
    n, ng = mesh.shape["gx"], mesh.shape["gy"]
    slots = P(("gx", "gy"), None)
    cube = P(("gx", "gy"), None, None)
    grid = P("gy", "gx")
    return jax.shard_map(
        functools.partial(on_device, n, ng),
        mesh=mesh,
        in_specs=(cube, cube, slots, P(), P(("gx", "gy")), slots, grid),
        out_specs=(cube, cube, grid, grid),
        check_vma=False,
    )
```

```python
import functools

import jax
import jax.numpy as jnp
from jax import lax
from jax.experimental import pallas as pl
from jax.experimental.pallas import tpu as pltpu
from jax.sharding import PartitionSpec as P

SPAN_E = 60
SPAN_N = 50
KX = 3
KY = 6
LEVELS = 30
SLOTS = KX * KY
CELLS = SPAN_E * SPAN_N
ROWS = KY * SPAN_N
COLS = KX * SPAN_E
TILES = 24
HALINE = 0.8
THERMAL = 0.6
DAMPING = 0.05

BIG = 56 * 2**20
TOP = 16
PLANE = 328
UROWS = TOP + SPAN_N * 8
BLK = 32
EAST = COLS - 128
MESH = pl.DeviceIdType.MESH
F32 = jnp.float32
I32 = jnp.int32
VMEM = pltpu.VMEM


def iota(shape, dim):
    return lax.broadcasted_iota(I32, shape, dim)


def lroll(x, shift):
    shift = shift % x.shape[1]
    return x if shift == 0 else pltpu.roll(x, shift, 1)


def sroll(x, shift):
    shift = shift % x.shape[0]
    return x if shift == 0 else pltpu.roll(x, shift, 0)


def lreverse(x):
    lane = iota(x.shape, 1)
    bit = 1
    while bit < 128:
        x = jnp.where((lane & bit) != 0, lroll(x, bit), lroll(x, -bit))
        bit *= 2
    return x


def flip_cols(a, b):
    ra, rb = lreverse(b), lreverse(a)
    shift = 256 - COLS
    lane = iota(a.shape, 1)
    xa, xb = lroll(ra, -shift), lroll(rb, -shift)
    return jnp.where(lane < 128 - shift, xa, xb), jnp.where(lane < 128 - shift, xb, xa)


def message_rows(cap):
    return cap * TILES + (cap * 3 + 7) // 8 * 8


def greet(peers):
    sem = pltpu.get_barrier_semaphore()
    for peer in peers:
        pl.semaphore_signal(sem, inc=1, device_id=peer, device_id_type=MESH)
    return lambda: pl.semaphore_wait(sem, len(peers))


class Exchange:
    def __init__(self, n, ng, g, y, row_out, row_in, col_out, col_in, row_s, row_r, col_s, col_r):
        self.n, self.ng, self.g, self.y = n, ng, g, y
        self.row_out, self.row_in, self.col_out, self.col_in = row_out, row_in, col_out, col_in
        self.row_s, self.row_r, self.col_s, self.col_r = row_s, row_r, col_s, col_r
        self.lane, self.sub = iota((8, 128), 1), iota((8, 128), 0)
        self.top = lax.div(y + 1, ng)

    def copies(self, k):
        n, ng, g, y, top = self.n, self.ng, self.g, self.y, self.top
        center = g + top * (n - 1 - 2 * g)
        result = []
        for place, d in ((0, 0), (1, 1), (2, -1)):
            target = lax.rem(center + d + n, n)
            up = pltpu.make_async_remote_copy(
                self.row_out.at[k, 0], self.row_in.at[k, top, place], self.row_s.at[k, 0, place],
                self.row_r.at[k, top, place], device_id=(target, y + 1 - top), device_id_type=MESH,
            )
            down, under = [
                pltpu.make_async_remote_copy(
                    self.row_out.at[k, 1], self.row_in.at[k, into, place], self.row_s.at[k, 1, place],
                    self.row_r.at[k, into, place],
                    device_id=(lax.rem(g + d + n, n), lax.rem(y + ng - 1, ng)), device_id_type=MESH,
                )
                for into in (1, 0)
            ]
            mine = None if d == 0 else (y == ng - 1) & (target == g)
            result.append((place, up, down, under, mine))
        cols = [
            pltpu.make_async_remote_copy(
                self.col_out.at[k, slot], self.col_in.at[k, slot], self.col_s.at[k, slot], self.col_r.at[k, slot],
                device_id=(target, y), device_id_type=MESH,
            )
            for slot, target in ((0, lax.rem(g + 1, n)), (1, lax.rem(g + n - 1, n)))
        ]
        return result, cols

    def pack(self, k, plane, caps=None):
        lane, sub = self.lane, self.sub
        north = [plane[half, 312:320, :] for half in range(2)]
        south = [plane[half, 16:24, :] for half in range(2)]
        turned = [
            jnp.where(
                sub < 2,
                jnp.where(sub == 0, sroll(v, -3), sroll(v, -1)),
                jnp.where(sub == 2, sroll(v, 1), sroll(v, 3)),
            )
            for v in north
        ]
        if caps is not None:
            for half in range(2):
                north[half] = jnp.where(sub == 5, caps[0][half], north[half])
                turned[half] = jnp.where(sub == 5, caps[0][half], turned[half])
                south[half] = jnp.where(sub == 5, caps[1][half], south[half])
        flipped = list(flip_cols(*turned))
        flipped[1] = jnp.where(
            lane == 60, lroll(turned[1], -1), jnp.where(lane == 61, lroll(turned[1], 1), flipped[1])
        )
        for half in range(2):
            self.row_out[k, 0, half] = jnp.where(self.y == self.ng - 1, flipped[half], north[half])
            self.row_out[k, 1, half] = south[half]
        for part in range(2):
            to_east = jnp.zeros((8, 128), F32)
            to_west = jnp.zeros((8, 128), F32)
            for t in range(32 * part, min(39, 32 * part + 32)):
                first = 4 * (t - 32 * part)
                here = (lane >= first) & (lane < first + 4)
                rows = slice(8 + 8 * t, 16 + 8 * t)
                a, b = plane[0, rows, :], plane[1, rows, :]
                east, west = lroll(b, first - (EAST - 4)), lroll(a, first)
                if caps is not None:
                    east = jnp.where(lane == first + 3, lroll(b, first + 3 - 60), lroll(b, first - (EAST - 3)))
                    west = jnp.where(lane == first + 3, lroll(b, first + 3 - 61), west)
                to_east = jnp.where(here, east, to_east)
                to_west = jnp.where(here, west, to_west)
            if part == 1 and caps is not None:
                here = (lane >= 64) & (lane < 67)
                both = [jnp.where(sub == 0, caps[0][half], caps[1][half]) for half in range(2)]
                to_east = jnp.where(here, lroll(both[1], 64 - (EAST - 3)), to_east)
                to_west = jnp.where(here, lroll(both[0], 64), to_west)
            self.col_out[k, 0, 8 * part : 8 * part + 8, :] = to_east
            self.col_out[k, 1, 8 * part : 8 * part + 8, :] = to_west

    def start(self, k):
        rows, cols = self.copies(k)
        for copy in cols:
            copy.start()
        for place, up, down, under, mine in rows:
            if mine is None:
                up.start()
            else:

                @pl.when(jnp.logical_not(mine))
                def _(up=up):
                    up.start()

                @pl.when(mine)
                def _(place=place):
                    self.row_in[k, 1, place] = self.row_out[k, 0]

            @pl.when(self.y > 0)
            def _(down=down):
                down.start()

        return rows, cols

    def wait(self, k, started):
        rows, cols = started
        for copy in cols:
            copy.wait()
        for place, up, down, under, mine in rows:
            if mine is None:
                up.wait_send()
                down.wait_recv()
            else:

                @pl.when(jnp.logical_not(mine))
                def _(up=up, down=down):
                    up.wait_send()
                    down.wait_recv()

            @pl.when(self.y > 0)
            def _(down=down, under=under):
                down.wait_send()
                under.wait_recv()

            @pl.when(self.y == 0)
            def _(place=place):
                self.row_in[k, 0, place] = jnp.zeros((2, 8, 128), F32)

    def unpack(self, k, plane, caps=None):
        lane, sub = self.lane, self.sub
        for part in range(2):
            west = self.col_in[k, 0, 8 * part : 8 * part + 8, :]
            east = self.col_in[k, 1, 8 * part : 8 * part + 8, :]
            for t in range(max(1, 32 * part), min(39, 32 * part + 32)):
                first = 4 * (t - 32 * part)
                rows = slice(8 + 8 * t, 16 + 8 * t)
                value = plane[1, rows, :]
                if caps is None:
                    value = jnp.where(lane >= 124, lroll(west, 124 - first), value)
                    value = jnp.where((lane >= EAST) & (lane < EAST + 4), lroll(east, EAST - first), value)
                else:
                    value = jnp.where(lane >= 125, lroll(west, 125 - first), value)
                    value = jnp.where((lane >= EAST) & (lane < EAST + 3), lroll(east, EAST - first), value)
                    value = jnp.where(lane == 62, lroll(east, 62 - first - 3), value)
                    value = jnp.where(lane == 63, lroll(west, 63 - first - 3), value)
                plane[1, rows, :] = value
        found = []
        for side in range(2):
            c, w, e = [[self.row_in[k, side, place, half] for half in range(2)] for place in range(3)]
            tail = jnp.where(lane >= 124, lroll(w[1], 76), c[1])
            tail = jnp.where((lane >= EAST) & (lane < EAST + 4), lroll(e[0], EAST), tail)
            tail = jnp.where(lane == 62, lroll(e[1], 1), jnp.where(lane == 63, lroll(w[1], 3), tail))
            found.append((c[0], tail))
        for half in range(2):
            plane[half, 8:16, :] = sroll(found[0][half], 4)
            plane[half, 312:320, :] = jnp.where(sub < 4, plane[half, 312:320, :], sroll(found[1][half], 4))
        if caps is None:
            return
        west, east = self.col_in[k, 0, 8:16, :], self.col_in[k, 1, 8:16, :]
        line = lane[0:1]
        for half in range(2):
            for which, row in ((0, 316), (1, 15)):
                value = caps[which][half]
                if half == 1:
                    value = jnp.where(line >= 125, lroll(west, 125 - 64)[which : which + 1], value)
                    value = jnp.where(
                        (line >= EAST) & (line < EAST + 3), lroll(east, EAST - 64)[which : which + 1], value
                    )
                plane[half, row : row + 1, :] = plane[half, row : row + 1, :] + value
            for side, row in ((1, 315), (0, 16)):
                value = found[side][half][5:6]
                if half == 1:
                    value = jnp.where((line < EAST + 3) | (line >= 125), value, 0.0)
                plane[half, row : row + 1, :] = plane[half, row : row + 1, :] + value


IDS = 36
MIRROR = 37
SIBLING = 40
OTHER = 48
STRIP_ROWS = 56


def strips_kernel(n, ng, cap, ids_ref, dfac_ref, depth_hbm, slot_hbm, flux_hbm,
                  all_ref, tab_ref, dpl, coef, nflat, fflat,
                  depth_ref, slot_ref, flux_ref, wide, msg, edge, got,
                  row_out, row_in, col_out, col_in,
                  own, s1, r1, s2, r2, s3, r3, row_s, row_r, col_s, col_r):
    g = lax.axis_index("gx")
    y = lax.axis_index("gy")
    loads = [
        pltpu.make_async_copy(src, dst, own.at[k])
        for k, (src, dst) in enumerate(((depth_hbm, depth_ref), (slot_hbm, slot_ref), (flux_hbm, flux_ref)))
    ]
    for load in loads:
        load.start()
    odd = lax.rem(y, 2)
    sibling = y + 1 - 2 * odd
    other = lax.rem(y + ng + 2 * odd - 1, ng)
    band = [(lax.rem(g + k, n), y) for k in range(1, n)]
    beside = [(lax.rem(g + k, n), other) for k in range(n)]
    corners = [(lax.rem(g + k, n), sibling) for k in (0, 1, n - 1)]
    everyone = greet(band + beside + corners)
    exchange = Exchange(n, ng, g, y, row_out, row_in, col_out, col_in, row_s, row_r, col_s, col_r)
    lane = iota((8, 128), 1)
    row = iota((1, 128), 1)
    code = jnp.full((1, 128), -1, I32)
    owners = []
    for s in range(SLOTS):
        block = jnp.maximum(ids_ref[s], 0)
        bx = lax.rem(block, KX * n)
        by = lax.rem(lax.div(block, KX * n), KY)
        owner = jnp.where(ids_ref[s] >= 0, lax.div(bx, KX), -1)
        rank = jnp.int32(0)
        for other in owners:
            rank = rank + jnp.where(other == owner, 1, 0)
        owners.append(owner)
        value = (owner * 32 + by * KX + lax.rem(bx, KX)) * 32 + rank
        code = jnp.where(row == s, jnp.where(owner >= 0, value, -1), code)
    loads[0].wait()
    for half in range(2):
        dpl[half, 0:16, :] = jnp.zeros((16, 128), F32)
        dpl[half, 312:UROWS, :] = jnp.zeros((UROWS - 312, 128), F32)
    wide[...] = jnp.zeros(wide.shape, F32)
    wide[0:COLS, 0:ROWS] = depth_ref[...].astype(F32)
    for half in range(2):
        for third in range(3):
            turned = wide[128 * half : 128 * half + 128, 128 * third : 128 * third + 128].T
            rows = min(128, ROWS - 128 * third)
            dpl[half, TOP + 128 * third : TOP + 128 * third + rows, :] = turned[0:rows]
    rims = [jnp.zeros((8, 128), F32) for _ in range(KX)]
    ns = []
    for i in range(SPAN_N):
        off = SPAN_E * i % 128
        a = dpl[0, pl.ds(TOP + i, 8, stride=SPAN_N), :]
        b = dpl[1, pl.ds(TOP + i, 8, stride=SPAN_N), :]
        cells = [a, a, jnp.where(lane < 64, b, a)]
        push = 0 if i < 32 else 1
        first, last = (off + push) % 128, (off + SPAN_E - 1 - push) % 128
        for bx in range(KX):
            turn = off - SPAN_E * bx
            rims[bx] = jnp.where(lane == first, lroll(cells[bx], turn + push), rims[bx])
            rims[bx] = jnp.where(lane == last, lroll(cells[bx], turn - push), rims[bx])
        if i == 0:
            ns = [lroll(cells[bx], -SPAN_E * bx) for bx in range(KX)]
        if i == SPAN_N - 1:
            ns = [
                jnp.where(lane < SPAN_E, ns[bx], lroll(cells[bx], SPAN_E - SPAN_E * bx))
                for bx in range(KX)
            ]
    ns = [v.astype(I32) for v in ns]
    for bx in range(KX):
        for part, value in enumerate((rims[bx].astype(I32), ns[bx])):
            msg[pl.ds(bx * 2 + part, 8, stride=6), :] = value
    msg[IDS : IDS + 1, :] = code
    edge[...] = jnp.zeros((8, 128), I32)
    for bx in range(KX):
        msg[MIRROR + bx : MIRROR + bx + 1, :] = lroll(lreverse(ns[bx]), -8)[KY - 1 : KY]
        edge[bx : bx + 1, :] = ns[bx][0:1]
        edge[3 + bx : 4 + bx, :] = ns[bx][KY - 1 : KY]
    exchange.pack(0, dpl)

    everyone()
    near = pltpu.make_async_remote_copy(
        edge, got, s1.at[0], r1.at[0], device_id=(g, sibling), device_id_type=MESH
    )
    near.start()
    sends = []
    for k, peer in enumerate(beside):
        copy = pltpu.make_async_remote_copy(
            edge, all_ref.at[g, pl.ds(OTHER, 8)], s3.at[k], r3.at[k], device_id=peer, device_id_type=MESH
        )
        copy.start()
        sends.append(copy)
    near.wait()
    msg[SIBLING : SIBLING + 8, :] = got[...]
    for k, peer in enumerate(band):
        copy = pltpu.make_async_remote_copy(
            msg, all_ref.at[g, pl.ds(0, OTHER)], s2.at[k], r2.at[k], device_id=peer, device_id_type=MESH
        )
        copy.start()
        sends.append(copy)
    halo = exchange.start(0)
    all_ref[pl.ds(g, 1), 0:OTHER] = msg[...][None]
    gain = jnp.zeros((1, 128), F32)
    for k in range(LEVELS):
        above = dfac_ref[k - 1] if k > 0 else jnp.float32(0)
        below = dfac_ref[k] if k + 1 < LEVELS else jnp.float32(0)
        base = (1.0 + above) - above * gain
        full = 1.0 / (base + below)
        gain = below * full
        coef[0, k : k + 1, :] = full
        coef[1, k : k + 1, :] = 1.0 / base
        coef[2, k : k + 1, :] = jnp.broadcast_to(above, (1, 128))
        coef[3, k : k + 1, :] = gain
    loads[1].wait()
    loads[2].wait()
    for t in range(TILES):
        width = min(128, CELLS - 128 * t)
        span = slice(t * 128, t * 128 + width)
        for first in (0, 8, 16):
            number = min(8, SLOTS - first)
            place = pl.ds(first * TILES + t, number, stride=TILES)
            for src, dst, kind in ((slot_ref, nflat, I32), (flux_ref, fflat, F32)):
                value = src[first : first + number, span]
                if width < 128:
                    value = jnp.concatenate([value, jnp.zeros((number, 128 - width), kind)], axis=1)
                dst[place, :] = value
    exchange.wait(0, halo)
    exchange.unpack(0, dpl)
    for copy in sends:
        copy.wait()
    codes = all_ref[:, IDS, :]
    key = codes >> 5
    rank = codes & 31
    source = iota((n, 128), 0)
    number = (source * cap + rank + 1).astype(F32)
    for p in range(SLOTS):
        hit = jnp.where(key == g * 32 + p, number, 0.0)
        hit = jnp.sum(jnp.sum(hit, axis=0, keepdims=True), axis=1, keepdims=True)
        tab_ref[p : p + 1, :] = jnp.broadcast_to(hit.astype(I32) - 1, (1, 128))
    tab_ref[SLOTS:24, :] = jnp.full((24 - SLOTS, 128), -1, I32)


def ahead(x, step):
    a = lroll(x, -step)
    return jnp.where(iota(x.shape, 1) < 128 - step, a, sroll(a, -1))


def behind(x, step):
    a = lroll(x, step)
    return jnp.where(iota(x.shape, 1) >= step, a, sroll(a, 1))


STEP = 33
AHEAD = 5


def columns_kernel(n, ng, cap, ids_ref, coef, fflat, nflat, strips_ref, heat_hbm, salt_hbm,
                   heat_out, salt_out, msg_ref, heat_in, salt_in, jcol, inh, ins, yh, ys, oh, os_, count, sems):
    step = pl.program_id(0)
    shape = (TILES, 128)
    row24 = iota(shape, 0)
    lane24 = iota(shape, 1)
    cell = row24 * 128 + lane24
    lane = iota((1, 128), 1)
    last = CELLS - 128 * (TILES - 1)

    ring = AHEAD + 1

    def loads(slot):
        place = lax.rem(slot, ring)
        return [
            pltpu.make_async_copy(src.at[slot], dst.at[place], sems.at[place, which])
            for which, (src, dst) in enumerate(((heat_hbm, heat_in), (salt_hbm, salt_in)))
        ]

    @pl.when(step == 0)
    def _():
        for slot in range(AHEAD):
            for load in loads(slot):
                load.start()
        flat = cell.astype(F32)
        whole = jnp.floor((flat + 0.5) * (1.0 / SPAN_E))
        jcol[...] = cell - whole.astype(I32) * SPAN_E
        for d in range(n):
            count[d] = 0

    @pl.when(step + AHEAD < SLOTS)
    def _():
        for load in loads(step + AHEAD):
            load.start()

    for load in loads(step):
        load.wait()
    here = lax.rem(step, ring)
    for t in range(TILES):
        width = 128 if t < TILES - 1 else last
        cols = slice(t * 128, t * 128 + width)
        inh[t * STEP : t * STEP + LEVELS, 0:width] = heat_in[here, :, cols]
        ins[t * STEP : t * STEP + LEVELS, 0:width] = salt_in[here, :, cols]

    mine = pl.ds(pl.multiple_of(step * TILES, 8), TILES)
    depth = nflat[mine, :]
    wet = depth > 0
    h = s = None
    for k in range(LEVELS):
        level = pl.ds(k, TILES, stride=STEP)
        rh = inh[level, :]
        rs = ins[level, :]
        deeper = depth > k + 1
        if k == 0:
            rh = rh + jnp.where(wet, fflat[mine, :], 0.0)
            pivot = jnp.where(deeper, coef[0, 0:1, :], 1.0)
            h = rh * pivot
            s = rs * pivot
        else:
            above = jnp.where(wet, coef[2, k : k + 1, :], 0.0)
            pivot = jnp.where(wet, coef[1, k : k + 1, :], 1.0)
            if k + 1 < LEVELS:
                pivot = jnp.where(deeper, coef[0, k : k + 1, :], pivot)
            h = (rh + above * h) * pivot
            s = (rs + above * s) * pivot
        if k + 1 < LEVELS:
            yh[k * TILES : (k + 1) * TILES, :] = h
            ys[k * TILES : (k + 1) * TILES, :] = s
        wet = deeper
    level = pl.ds(LEVELS - 1, TILES, stride=STEP)
    oh[level, :] = h
    os_[level, :] = s
    for k in range(LEVELS - 2, -1, -1):
        gain = jnp.where(depth > k + 1, coef[3, k : k + 1, :], 0.0)
        h = yh[k * TILES : (k + 1) * TILES, :] + gain * h
        s = ys[k * TILES : (k + 1) * TILES, :] + gain * s
        level = pl.ds(k, TILES, stride=STEP)
        oh[level, :] = h
        os_[level, :] = s
    for t in range(TILES):
        width = 128 if t < TILES - 1 else last
        cols = slice(t * 128, t * 128 + width)
        heat_out[0, :, cols] = oh[t * STEP : t * STEP + LEVELS, 0:width]
        salt_out[0, :, cols] = os_[t * STEP : t * STEP + LEVELS, 0:width]

    blocks_x = KX * n
    ident = ids_ref[step]
    block = jnp.maximum(ident, 0)
    bx = lax.rem(block, blocks_x)
    by = lax.div(block, blocks_x)
    byl = lax.rem(by, KY)
    dev = lax.div(bx, KX)
    bxl = lax.rem(bx, KX)

    def strip(device, place):
        return strips_ref[device, pl.ds(place, 1), :]

    def rim_of(col):
        return strip(lax.div(col, KX), (byl * KX + lax.rem(col, KX)) * 2)

    east = rim_of(lax.rem(bx + 1, blocks_x))
    west = rim_of(lax.rem(bx + blocks_x - 1, blocks_x))
    ew = [
        jnp.where((lane & 3) == 3, lroll(east, SPAN_E - 1 - push), lroll(west, 1 - SPAN_E + push))
        for push in range(2)
    ]
    ew = jnp.where(row24 < 15, ew[0], ew[1])
    mirror = blocks_x - 1 - bx
    mirrored = lax.rem(mirror, KX)
    folded = by == KY * ng - 1
    inner = byl < KY - 1
    even = lax.rem(lax.div(by, KY), 2) == 0
    north_dev = jnp.where(folded, lax.div(mirror, KX), dev)
    north_row = jnp.where(
        inner,
        ((byl + 1) * KX + bxl) * 2 + 1,
        jnp.where(folded, MIRROR + mirrored, jnp.where(even, SIBLING, OTHER) + bxl),
    )
    north = lroll(strip(north_dev, north_row), -4)
    south_row = jnp.where(byl > 0, ((byl - 1) * KX + bxl) * 2 + 1, jnp.where(even, OTHER, SIBLING) + 3 + bxl)
    south = jnp.where(by > 0, lroll(strip(dev, south_row), -SPAN_E), 0)
    j = jcol[...]
    inside = cell < CELLS
    first_j = j == 0
    last_j = j == SPAN_E - 1
    first_i = cell < SPAN_E
    last_i = cell >= CELLS - SPAN_E
    faces = (
        jnp.minimum(depth, jnp.where(last_j, ew, ahead(depth, 1))),
        jnp.minimum(depth, jnp.where(first_j, ew, behind(depth, 1))),
        jnp.minimum(depth, jnp.where(last_i, north, ahead(depth, SPAN_E))),
        jnp.minimum(depth, jnp.where(first_i, south, behind(depth, SPAN_E))),
    )
    sums = [jnp.zeros(shape, F32) for _ in range(4)]
    pressure = jnp.zeros(shape, F32)
    total = jnp.zeros(shape, F32)
    for k in range(LEVELS):
        level = pl.ds(k, TILES, stride=STEP)
        pressure = pressure + (HALINE * os_[level, :] - THERMAL * oh[level, :])
        total = total + pressure
        sums = [jnp.where(face == k + 1, total, held) for face, held in zip(faces, sums)]
    sums = [jnp.where(inside, held, 0.0) for held in sums]
    se, sw, sn, ss = sums
    local = jnp.where(last_j, 0.0, ahead(sw, 1)) - se
    local = local + (jnp.where(first_j, 0.0, behind(se, 1)) - sw)
    local = local + (jnp.where(last_i, 0.0, ahead(ss, SPAN_E)) - sn)
    local = local + (jnp.where(first_i, 0.0, behind(sn, SPAN_E)) - ss)
    local = jnp.where(inside, local, 0.0)
    rim = jnp.where(last_j, se, jnp.where(first_j, sw, 0.0))
    rim0 = jnp.sum(jnp.where(row24 < 15, rim, 0.0), axis=0, keepdims=True)
    rim1 = jnp.sum(jnp.where(row24 >= 15, rim, 0.0), axis=0, keepdims=True)
    top = jnp.sum(jnp.where(last_i, sn, 0.0), axis=0, keepdims=True)
    bottom = jnp.sum(jnp.where(first_i, ss, 0.0), axis=0, keepdims=True)
    cap_row = jnp.where(lane < SPAN_E, bottom, jnp.where(lane < 2 * SPAN_E, lroll(top, 64), 0.0))

    @pl.when(ident >= 0)
    def _():
        rank = count[dev]
        count[dev] = rank + 1
        msg_ref[dev, pl.ds(pl.multiple_of(rank * TILES, 8), TILES), :] = local
        base = cap * TILES + rank * 3
        for part, value in enumerate((rim0, rim1, cap_row)):
            msg_ref[dev, pl.ds(base + part, 1), :] = value


def barotropic_kernel(n, ng, cap, tab_ref, dpl, msg_ref, height_ref, misfit_ref,
                      recv, blk, upl, zs, spare, wts, qpl, row_out, row_in, col_out, col_in,
                      red_out, red_x, red_y, own_sem, a2a_s, a2a_r, row_s, row_r, col_s, col_r,
                      rx_s, rx_r, ry_s, ry_r):
    g = lax.axis_index("gx")
    y = lax.axis_index("gy")
    band = [(lax.rem(g + k, n), y) for k in range(1, n)]
    column = [(g, lax.rem(y + k, ng)) for k in range(1, ng)]
    corners = [(lax.rem(g + a, n), lax.rem(y + b, ng)) for a in (1, n - 1) for b in (1, ng - 1)]
    everyone = greet(band + column + corners)
    exchange = Exchange(n, ng, g, y, row_out, row_in, col_out, col_in, row_s, row_r, col_s, col_r)
    lane = iota((8, 128), 1)
    sub = iota((8, 128), 0)
    zero8 = jnp.zeros((8, 128), F32)
    for half in range(2):
        for ref in (zs.at[0], zs.at[1], zs.at[2]):
            ref[half, 0:8, :] = zero8
            ref[half, 320:PLANE, :] = zero8

    span = 24
    chunks = 13
    lane_c = iota((span, 128), 1)

    def rows_at(t, shift=0):
        return pl.ds(8 + t * span + shift, span)

    def both(ref, rows):
        return [ref[half, rows, :] for half in range(2)]

    def from_east(pair):
        a, b = [lroll(v, -1) for v in pair]
        return jnp.where(lane_c < 127, a, b), jnp.where(lane_c < 127, b, a)

    def from_west(pair):
        a, b = [lroll(v, 1) for v in pair]
        return jnp.where(lane_c >= 1, a, b), jnp.where(lane_c >= 1, b, a)

    def weigh(t, carry):
        rows = rows_at(t)
        d = both(dpl, rows)
        beside = (from_east(d), from_west(d), both(dpl, rows_at(t, 1)), both(dpl, rows_at(t, -1)))
        r = iota((span, 128), 0) + (8 + t * span)
        for half in range(2):
            damp = jnp.where(d[half] > 0, DAMPING, 1.0)
            diagonal = damp
            for side in range(4):
                w = jnp.minimum(d[half], beside[side][half]) * (1.0 / LEVELS)
                wts[side, half, rows, :] = w
                diagonal = diagonal + w
            inverse = 1.0 / diagonal
            wts[4, half, rows, :] = damp
            wts[5, half, rows, :] = inverse
            inside = (r >= TOP) & (r < TOP + ROWS)
            if half == 1:
                inside = inside & (lane_c < EAST)
            wts[6, half, rows, :] = jnp.where(inside, inverse, 0.0)
        return carry

    lax.fori_loop(0, chunks, weigh, 0, unroll=True)

    everyone()
    own = pltpu.make_async_copy(msg_ref.at[g], recv.at[g], own_sem)
    own.start()
    sends = []
    for k, peer in enumerate(band):
        copy = pltpu.make_async_remote_copy(
            msg_ref.at[peer[0]], recv.at[g], a2a_s.at[k], a2a_r.at[k], device_id=peer, device_id_type=MESH
        )
        copy.start()
        sends.append(copy)


    own.wait()
    for copy in sends:
        copy.wait()
    for bx in range(KX):
        blk[(bx * 8 + KY) * BLK : (bx + 1) * 8 * BLK, :] = jnp.zeros((2 * BLK, 128), F32)
        wanted = [
            jnp.broadcast_to(tab_ref[by * KX + bx : by * KX + bx + 1, :], (8, 128)) for by in range(KY)
        ]

        def pick(source, held, wanted=wanted):
            held = list(held)
            for rank in range(cap):
                parts = [recv[source, rank * TILES + 8 * v : rank * TILES + 8 * v + 8, :] for v in range(3)]
                first = cap * TILES + rank * 3
                rest = recv[source, first : first + 3, :]
                for by in range(KY):
                    hit = wanted[by] == source * cap + rank
                    for v in range(3):
                        held[by * 4 + v] = jnp.where(hit, parts[v], held[by * 4 + v])
                    held[by * 4 + 3] = jnp.where(hit[0:3], rest, held[by * 4 + 3])
            return tuple(held)

        start = ([zero8] * 3 + [jnp.zeros((3, 128), F32)]) * KY
        held = lax.fori_loop(0, n, pick, tuple(start))
        for by in range(KY):
            base = (bx * 8 + by) * BLK
            for v in range(3):
                blk[base + 8 * v : base + 8 * v + 8, :] = held[by * 4 + v]
            blk[base + TILES : base + TILES + 3, :] = held[by * 4 + 3]

    def rows_of(bx, row):
        return blk[pl.ds(bx * 8 * BLK + row, 8, stride=BLK), :]

    rims = [[rows_of(bx, TILES + part) for part in range(2)] for bx in range(KX)]
    cap_rows = [rows_of(bx, TILES + 2) for bx in range(KX)]

    def lay(v):
        tail = jnp.where(lane < EAST, v[2], 0.0)
        return jnp.where(lane < 60, v[0], jnp.where(lane < 120, v[1], v[2])), tail

    souths = lay([lroll(cap_rows[bx], SPAN_E * bx) for bx in range(KX)])
    norths = lay([lroll(cap_rows[bx], SPAN_E * bx - SPAN_E) for bx in range(KX)])
    for i in range(SPAN_N):
        t, off = SPAN_E * i // 128, SPAN_E * i % 128
        cells = []
        for bx in range(KX):
            value = rows_of(bx, t)
            if off + SPAN_E > 128:
                value = jnp.where(lane >= off, value, rows_of(bx, t + 1))
            cells.append(lroll(value, SPAN_E * bx - off))
        first, second = lay(cells)
        second = jnp.where(
            lane == 60,
            lroll(rims[KX - 1][i // 32], 61 - SPAN_E - off),
            jnp.where(lane == 61, lroll(rims[0][i // 32], 61 - off), second),
        )
        rim = [rims[bx][i // 32] for bx in range(KX)]
        first = first + jnp.where(
            lane == 59,
            lroll(rim[1], 59 - off),
            jnp.where(
                lane == 60,
                lroll(rim[0], 1 - off),
                jnp.where(lane == 119, lroll(rim[2], 119 - off), jnp.where(lane == 120, lroll(rim[1], 61 - off), 0.0)),
            ),
        )
        if i == SPAN_N - 1:
            first = first + jnp.where(sub < KY - 1, sroll(souths[0], -1), 0.0)
            second = second + jnp.where(sub < KY - 1, sroll(souths[1], -1), 0.0)
        if i == 0:
            first = first + jnp.where((sub > 0) & (sub < KY), sroll(norths[0], 1), 0.0)
            second = second + jnp.where((sub > 0) & (sub < KY), sroll(norths[1], 1), 0.0)
        upl[0, pl.ds(TOP + i, 8, stride=SPAN_N), :] = first
        upl[1, pl.ds(TOP + i, 8, stride=SPAN_N), :] = second
    for half in range(2):
        upl[half, 8:16, :] = zero8
    caps = ([v[KY - 1 : KY] for v in norths], [v[0:1] for v in souths])
    exchange.pack(0, upl, caps)
    exchange.wait(0, exchange.start(0))
    exchange.unpack(0, upl, caps)

    def begin(t, carry):
        rows = rows_at(t)
        a, b = both(upl, rows)
        a = a + jnp.where(lane_c == 0, lroll(b, -63), 0.0)
        b = b + jnp.where(
            lane_c == EAST - 1,
            lroll(b, EAST - 1 - 62),
            jnp.where(lane_c == EAST, lroll(b, EAST - 60), jnp.where(lane_c == 127, lroll(b, 127 - 61), 0.0)),
        )
        for half, value in enumerate((a, b)):
            rhs = value * (1.0 / LEVELS)
            qpl[0, half, rows, :] = rhs
            zs[0, half, rows, :] = rhs * wts[5, half, rows, :]
        return carry

    lax.fori_loop(0, chunks, begin, 0, unroll=True)

    def image(out):
        z = zs.at[out - 1]

        def body(t, carry):
            rows = rows_at(t)
            v = both(z, rows)
            beside = (from_east(v), from_west(v), both(z, rows_at(t, 1)), both(z, rows_at(t, -1)))
            for half in range(2):
                result = wts[4, half, rows, :] * v[half]
                for side in range(4):
                    result = result + wts[side, half, rows, :] * (v[half] - beside[side][half])
                qpl[out, half, rows, :] = result
                if out < 3:
                    zs[out, half, rows, :] = result * wts[5, half, rows, :]
            return carry

        lax.fori_loop(0, chunks, body, 0, unroll=True)

    image(1)
    image(2)
    image(3)

    def fold3(v):
        return v[0:8] + v[8:16] + v[16:24]

    def first_dots(t, carry):
        rows = rows_at(t)
        a, b = carry
        for half in range(2):
            z = qpl[0, half, rows, :] * wts[6, half, rows, :]
            a = a + fold3(qpl[0, half, rows, :] * z)
            b = b + fold3(qpl[1, half, rows, :] * z)
        return a, b

    def splat(v):
        v = jnp.sum(jnp.sum(v, axis=0, keepdims=True), axis=1, keepdims=True)
        return jnp.broadcast_to(v, (8, 128))

    mass, curve = [splat(v) for v in lax.fori_loop(0, chunks, first_dots, (zero8, zero8), unroll=True)]
    own_ray = jnp.where(mass > 0, jnp.clip(curve / jnp.where(mass > 0, mass, 1.0), 0.0, 2.0), 0.0)
    ray_c = jnp.broadcast_to(own_ray[0:1], (span, 128))
    pairs = ((0, 0), (1, 0), (2, 0), (3, 0), (1, 1), (2, 1), (3, 1), (2, 2), (3, 2))

    def shift(t, carry):
        rows = rows_at(t)
        c = list(carry)
        for half in range(2):
            w0, w1, w2, w3 = [qpl[j, half, rows, :] for j in range(4)]
            q1 = w1 - ray_c * w0
            t2 = w2 - ray_c * w1
            t3 = (w3 - ray_c * w2) - ray_c * t2
            q2 = t2 - ray_c * q1
            q3 = t3 - ray_c * q2
            qpl[1, half, rows, :] = q1
            qpl[2, half, rows, :] = q2
            qpl[3, half, rows, :] = q3
            q = (w0, q1, q2, q3)
            inverse = wts[6, half, rows, :]
            z = [v * inverse for v in q[0:3]]
            for place, (i, j) in enumerate(pairs):
                c[place] = c[place] + fold3(q[i] * z[j])
        return tuple(c)

    sums = lax.fori_loop(0, chunks, shift, (zero8,) * len(pairs), unroll=True)
    red_out[0, 0:1, :] = own_ray[0:1]
    red_out[0, 1:2, :] = mass[0:1]
    for place, part in enumerate(sums):
        red_out[0, 2 + place : 3 + place, :] = jnp.sum(part, axis=0, keepdims=True)
    red_out[0, 11:16, :] = jnp.zeros((5, 128), F32)
    for level, (peers, into, sem_s, sem_r, me) in enumerate(
        ((band, red_x, rx_s, rx_r, g), (column, red_y, ry_s, ry_r, y))
    ):
        place = pl.ds(pl.multiple_of(me * 16, 8), 16)
        copies = []
        for number, peer in enumerate(peers):
            copy = pltpu.make_async_remote_copy(
                red_out.at[level], into.at[place], sem_s.at[number], sem_r.at[number],
                device_id=peer, device_id_type=MESH,
            )
            copy.start()
            copies.append(copy)
        into[place, :] = red_out[level]
        for copy in copies:
            copy.wait()
        count = len(peers) + 1
        ray, mass, *old = [into[pl.ds(m, count, stride=16), :] for m in range(2 + len(pairs))]
        total = jnp.sum(mass, axis=0, keepdims=True)
        common = jnp.sum(ray * mass, axis=0, keepdims=True) / total
        common = jnp.where(total > 0, common, 0.0)
        d = ray - common
        terms = [[None] * 4 for _ in range(4)]
        for i, c in enumerate(((1,), (1, 1), (1, 2, 1), (1, 3, 3, 1))):
            for j in range(i + 1):
                power = jnp.full(d.shape, float(c[j]), F32)
                for _ in range(i - j):
                    power = power * d
                terms[i][j] = power
        gram = dict(zip(pairs, old))

        def entry(i, j):
            return gram[(i, j)] if i >= j else gram[(j, i)]

        new = []
        for i, j in pairs:
            value = None
            for a in range(i + 1):
                for b in range(j + 1):
                    term = entry(a, b)
                    if a < i:
                        term = term * terms[i][a]
                    if b < j:
                        term = term * terms[j][b]
                    value = term if value is None else value + term
            new.append(jnp.sum(value, axis=0, keepdims=True))
        if level == 0:
            red_out[1, 0:1, :] = common
            red_out[1, 1:2, :] = total
            for number, part in enumerate(new):
                red_out[1, 2 + number : 3 + number, :] = part
            red_out[1, 11:16, :] = jnp.zeros((5, 128), F32)
    ray = jnp.broadcast_to(common, (8, 128))
    moment = {
        pair: jnp.broadcast_to(jnp.sum(part, axis=1, keepdims=True), (8, 128)) for pair, part in zip(pairs, new)
    }
    norm = moment[(0, 0)]
    moment = [moment[pair] for pair in ((1, 0), (1, 1), (2, 1), (2, 2), (3, 2))]
    one = jnp.ones((8, 128), F32)
    scale = one / norm
    c = [one] + [m * scale for m in moment]
    zero = zero8
    rho = [one, zero, zero, zero]
    pi = [one, zero, zero]
    xs = [zero, zero, zero]
    gamma = one
    for it in range(3):
        curve = zero
        for i in range(it + 1):
            for j in range(it + 1):
                curve = curve + (pi[i] * pi[j]) * (ray * c[i + j] + c[i + j + 1])
        alpha = gamma / curve
        xs = [xs[i] + alpha * pi[i] if i <= it else xs[i] for i in range(3)]
        for i in range(it + 2):
            step = ray * pi[i] if i <= it else zero
            if i > 0:
                step = step + pi[i - 1]
            rho[i] = rho[i] - alpha * step
        if it == 2:
            break
        gamma_new = zero
        for i in range(it + 2):
            for j in range(it + 2):
                gamma_new = gamma_new + (rho[i] * rho[j]) * c[i + j]
        beta = gamma_new / gamma
        pi = [rho[i] + beta * pi[i] for i in range(3)]
        gamma = gamma_new

    d = own_ray - ray
    d2 = d * d
    rho = [
        rho[0] + d * rho[1] + d2 * rho[2] + d2 * d * rho[3],
        rho[1] + 2.0 * d * rho[2] + 3.0 * d2 * rho[3],
        rho[2] + 3.0 * d * rho[3],
        rho[3],
    ]
    xs = [xs[0] + d * xs[1] + d2 * xs[2], xs[1] + 2.0 * d * xs[2], xs[2]]

    def finish(first, size):
        rows = pl.ds(TOP + first, size)
        x = [jnp.broadcast_to(v[0:1], (size, 128)) for v in xs]
        r = [jnp.broadcast_to(v[0:1], (size, 128)) for v in rho]
        for half in range(2):
            q = [qpl[j, half, rows, :] for j in range(4)]
            high = (x[0] * q[0] + x[1] * q[1] + x[2] * q[2]) * wts[5, half, rows, :]
            rest = r[0] * q[0] + r[1] * q[1] + r[2] * q[2] + r[3] * q[3]
            spare[half, rows, :] = high
            upl[half, rows, :] = rest

    def finish_chunk(t, carry):
        finish(pl.multiple_of(t * span, 8), span)
        return carry

    lax.fori_loop(0, ROWS // span, finish_chunk, 0, unroll=True)
    finish(ROWS // span * span, ROWS % span)
    for source, out_ref in ((spare, height_ref), (upl, misfit_ref)):
        for half in range(2):
            for third in range(3):
                turned = source[half, TOP + 128 * third : TOP + 128 * third + 128, :].T
                tall, wide = min(128, COLS - 128 * half), min(128, ROWS - 128 * third)
                out_ref[128 * half : 128 * half + tall, 128 * third : 128 * third + wide] = turned[0:tall, 0:wide]


def place_kernel(a_ref, b_ref, a_out, b_out):
    a_out[...] = a_ref[...]
    b_out[...] = b_ref[...]


def strips_call(n, ng, flux, dfac, ids, slot_depth, grid_depth):
    vmem = pl.BlockSpec(memory_space=VMEM)
    smem = pl.BlockSpec(memory_space=pltpu.SMEM)
    hbm = pl.BlockSpec(memory_space=pl.ANY)
    dma = pltpu.SemaphoreType.DMA
    flat = (SLOTS * TILES, 128)
    return pl.pallas_call(
        functools.partial(strips_kernel, n, ng, (SLOTS + n - 1) // n),
        out_shape=(
            jax.ShapeDtypeStruct((n, STRIP_ROWS, 128), I32), jax.ShapeDtypeStruct((24, 128), I32),
            jax.ShapeDtypeStruct((2, UROWS, 128), F32), jax.ShapeDtypeStruct((4, 32, 128), F32),
            jax.ShapeDtypeStruct(flat, I32), jax.ShapeDtypeStruct(flat, F32),
        ),
        in_specs=[smem, smem, hbm, hbm, hbm],
        out_specs=(vmem,) * 6,
        scratch_shapes=[
            VMEM((COLS, ROWS), I32), VMEM((SLOTS, CELLS), I32), VMEM((SLOTS, CELLS), F32),
            VMEM((256, 384), F32), VMEM((48, 128), I32), VMEM((8, 128), I32), VMEM((8, 128), I32),
            VMEM((1, 2, 2, 8, 128), F32), VMEM((1, 2, 3, 2, 8, 128), F32),
            VMEM((1, 2, 16, 128), F32), VMEM((1, 2, 16, 128), F32),
            dma((3,)), dma((1,)), dma((1,)), dma((n,)), dma((n,)), dma((n,)), dma((n,)),
            dma((1, 2, 3)), dma((1, 2, 3)), dma((1, 2)), dma((1, 2)),
        ],
        compiler_params=pltpu.CompilerParams(collective_id=0, has_side_effects=True, vmem_limit_bytes=BIG),
        name="strips",
    )(ids, dfac, grid_depth.T, slot_depth, flux)


def columns_call(n, ng, heat, salt, ids, coef, fflat, nflat, strips):
    cap = (SLOTS + n - 1) // n
    msg_rows = message_rows(cap)
    smem = pl.BlockSpec(memory_space=pltpu.SMEM)
    hbm = pl.BlockSpec(memory_space=pl.ANY)
    fixed = lambda shape: pl.BlockSpec(shape, lambda s: (0,) * len(shape))
    block = pl.BlockSpec((1, LEVELS, CELLS), lambda s: (s, 0, 0))
    ring = (AHEAD + 1, LEVELS, CELLS)
    tall = TILES * STEP + 8
    return pl.pallas_call(
        functools.partial(columns_kernel, n, ng, cap),
        grid=(SLOTS,),
        out_shape=(
            jax.ShapeDtypeStruct(heat.shape, F32),
            jax.ShapeDtypeStruct(salt.shape, F32),
            jax.ShapeDtypeStruct((n, msg_rows, 128), F32),
        ),
        in_specs=[
            smem, fixed((4, 32, 128)), fixed((SLOTS * TILES, 128)), fixed((SLOTS * TILES, 128)),
            fixed((n, STRIP_ROWS, 128)), hbm, hbm,
        ],
        out_specs=(block, block, fixed((n, msg_rows, 128))),
        scratch_shapes=[
            VMEM(ring, F32), VMEM(ring, F32), VMEM((TILES, 128), I32),
            VMEM((tall, 128), F32), VMEM((tall, 128), F32),
            VMEM((TILES * LEVELS, 128), F32), VMEM((TILES * LEVELS, 128), F32),
            VMEM((tall, 128), F32), VMEM((tall, 128), F32),
            pltpu.SMEM((n,), I32), pltpu.SemaphoreType.DMA((AHEAD + 1, 2)),
        ],
        compiler_params=pltpu.CompilerParams(vmem_limit_bytes=BIG),
        name="columns",
    )(ids, coef, fflat, nflat, strips, heat, salt)


def barotropic_call(n, ng, table, depths, msg):
    cap = (SLOTS + n - 1) // n
    vmem = pl.BlockSpec(memory_space=VMEM)
    dma = pltpu.SemaphoreType.DMA
    field = jax.ShapeDtypeStruct((COLS, ROWS), F32)
    plane = (2, PLANE, 128)
    return pl.pallas_call(
        functools.partial(barotropic_kernel, n, ng, cap),
        out_shape=(field, field),
        in_specs=[vmem, vmem, pl.BlockSpec(memory_space=pl.ANY)],
        out_specs=(vmem, vmem),
        scratch_shapes=[
            VMEM((n, message_rows(cap), 128), F32), VMEM((KX * 8 * BLK, 128), F32),
            VMEM((2, UROWS, 128), F32), VMEM((3,) + plane, F32), VMEM((2, UROWS, 128), F32),
            VMEM((7,) + plane, F32), VMEM((4,) + plane, F32),
            VMEM((1, 2, 2, 8, 128), F32), VMEM((1, 2, 3, 2, 8, 128), F32),
            VMEM((1, 2, 16, 128), F32), VMEM((1, 2, 16, 128), F32),
            VMEM((2, 16, 128), F32), VMEM((n * 16, 128), F32), VMEM((ng * 16, 128), F32),
            dma, dma((n,)), dma((n,)), dma((1, 2, 3)), dma((1, 2, 3)), dma((1, 2)), dma((1, 2)),
            dma((n,)), dma((n,)), dma((ng,)), dma((ng,)),
        ],
        compiler_params=pltpu.CompilerParams(collective_id=1, has_side_effects=True, vmem_limit_bytes=BIG),
        name="barotropic",
    )(table, depths, msg)


def on_device(n, ng, heat, salt, flux, dfac, ids, slot_depth, grid_depth):
    strips, table, depths, coef, nflat, fflat = strips_call(n, ng, flux, dfac, ids, slot_depth, grid_depth)
    heat_new, salt_new, msg = columns_call(n, ng, heat, salt, ids, coef, fflat, nflat, strips)
    height, misfit = barotropic_call(n, ng, table, depths, msg)
    vmem = pl.BlockSpec(memory_space=VMEM)
    field = jax.ShapeDtypeStruct((COLS, ROWS), F32)
    height, misfit = pl.pallas_call(
        place_kernel, out_shape=(field, field), in_specs=[vmem, vmem], out_specs=(vmem, vmem), name="place"
    )(height, misfit)
    return heat_new, salt_new, height.T, misfit.T


def solution(mesh):
    n, ng = mesh.shape["gx"], mesh.shape["gy"]
    slots = P(("gx", "gy"), None)
    cube = P(("gx", "gy"), None, None)
    grid = P("gy", "gx")
    return jax.shard_map(
        functools.partial(on_device, n, ng),
        mesh=mesh,
        in_specs=(cube, cube, slots, P(), P(("gx", "gy")), slots, grid),
        out_specs=(cube, cube, grid, grid),
        check_vma=False,
    )
```
